256 devices in a mesh: sub: 64 (over z, y, x_lo), fold: 4 (over x_hi, core).
Axes of the slice: x: 4 (x_hi: 2, x_lo: 2; x = x_hi * 2 + x_lo), y: 4, z: 8, core: 2. Of those that a mesh axis runs over, the one named last changes fastest.
Arguments:
- right_side: float32 [32768, 64], P(('sub', 'fold')), may hold values from -6 to 6
- blocks: float32 [256, 7, 128, 128], P('sub'), may hold values from -2 to 9, as said below
- block_cols: int32 [256, 7], P('sub'), may hold values from 0 to 7, as said below
- send_lists: int32 [64, 2, 2], P('sub'), may hold values from 0 to 3, as said below
Outputs:
- correction: float32 [32768, 64], P(('sub', 'fold'))
- residual: float32 [32768, 64], P(('sub', 'fold'))
The draws below stay inside these ranges and needn't reach their ends.
Inputs may be any that keep to these rules, and one draw needn't show every extreme that they name: `block_cols`: entry 0 of each block row is the row's own block (its device index). Values below 4 name the device's own blocks, 4 + j the j-th block of the previous device's list to its next neighbour, 6 + j the j-th block of the next device's list to its previous neighbour; the first subset device names no previous neighbour's block and the last none of the next. `send_lists`: each list holds 2 distinct block indices of the device's own blocks. `blocks`: the operator is nonsingular and well conditioned.
All inputs are finite; a program needn't handle non-finite values.
Results may differ from the reference program's by a relative error of at most 0.0003.
Values sent between devices are 32-bit elements; how exact they have to be, the bound alone decides.
No kernel may reach another device: no remote copies, remote signals or barrier semaphores. Data moves between devices by JAX's collectives and lax.ppermute only.
A program may use at most 64 MiB of HBM per device.

```python
import jax
import jax.numpy as jnp
from jax import lax

NB_DEV = 4
BS = 128
K = 7
HALO = 2
STEPS = 4
CYCLES = 3
NRHS = 64
NBLK = 256
ROWS = 32768
N_SUB = 64


def draw_blocks(key, part):
    key = jax.random.fold_in(key, 11)
    key_vals, key_diag, key_rows = jax.random.split(key, 3)
    scale = 1.0 / (K * BS) ** 0.5
    rough = jnp.exp(jax.random.uniform(key_rows, (NBLK, 1, BS, 1), jnp.float32, -0.69, 0.69))
    values = jnp.clip(jax.random.normal(key_vals, (NBLK, K, BS, BS), jnp.float32), -4.0, 4.0) * scale * rough
    diagonal = jax.random.uniform(key_diag, (NBLK, BS), jnp.float32, 1.5, 7.5)
    first = values[:, 0] + diagonal[:, :, None] * jnp.eye(BS, dtype=jnp.float32)[None]
    return values.at[:, 0].set(first)


def draw_block_cols(key, part):
    key = jax.random.fold_in(key, 12)
    row_ids = jnp.arange(NBLK, dtype=jnp.int32)
    device = row_ids // NB_DEV
    local = row_ids % NB_DEV
    left_ok = device > 0
    right_ok = device < N_SUB - 1
    random_cols = jax.random.randint(key, (NBLK, K), 0, NB_DEV + 2 * HALO, jnp.int32)
    is_left = (random_cols >= NB_DEV) & (random_cols < NB_DEV + HALO)
    is_right = random_cols >= NB_DEV + HALO
    barred = is_left & ~left_ok[:, None] | is_right & ~right_ok[:, None]
    random_cols = jnp.where(barred, random_cols % NB_DEV, random_cols)
    first_col = local
    second_col = jnp.where(left_ok, NB_DEV + local % HALO, (local + 1) % NB_DEV)
    third_col = jnp.where(right_ok, NB_DEV + HALO + local % HALO, (local + NB_DEV - 1) % NB_DEV)
    fixed_cols = jnp.stack([first_col, second_col, third_col], 1)
    return jnp.concatenate([fixed_cols, random_cols[:, 3:]], 1).astype(jnp.int32)


def draw_send_lists(key, part):
    key = jax.random.fold_in(key, 13)
    keys = jax.random.split(key, 2 * N_SUB)
    orders = jax.vmap(lambda one_key: jax.random.permutation(one_key, NB_DEV))(keys).astype(jnp.int32)
    first_row = (orders[0] + (NB_DEV - 1) - orders[0, 0]) % NB_DEV
    second_row = (orders[1] - orders[1, 0]) % NB_DEV
    orders = orders.at[0].set(first_row).at[1].set(second_row)
    return orders[:, :HALO].reshape(N_SUB, 2, HALO).astype(jnp.int32)


def block_scale(stream_key, extent, pieces, low, top_value):
    gain = 1.0
    for dim, shards_of in pieces:
        steps = jax.random.uniform(jax.random.fold_in(jax.random.fold_in(stream_key, 6), dim), (shards_of,), jnp.float32, low / len(pieces), top_value / len(pieces))
        gain = gain * jnp.repeat(jnp.exp(steps), extent[dim] // shards_of).reshape((-1,) + (1,) * (len(extent) - 1 - dim))
    return gain


def bell_draw(key, extent, spread, reach, cuts=(), held_as=jnp.bfloat16):
    entries = spread * jax.random.normal(key, extent, jnp.float32)
    if cuts:
        entries = entries * block_scale(key, extent, cuts, -0.22, 0.18)
    return jnp.clip(entries, -reach, reach).astype(held_as)


def setup_inputs(seed: int = 0) -> dict:
    key_list = jax.random.split(jax.random.key(seed), 5)
    return {
        "right_side": bell_draw(key_list[0], (ROWS, NRHS), 1.0, 6.0, ((0, 256),), jnp.float32),
        "blocks": draw_blocks(jax.random.fold_in(key_list[4], 71), 0),
        "block_cols": draw_block_cols(jax.random.fold_in(key_list[4], 71), 0),
        "send_lists": draw_send_lists(jax.random.fold_in(key_list[4], 71), 0),
    }


CENTER = 4.5
RADIUS = 3.5

def small_solve(matrix, target):
    count = matrix.shape[0]
    lower = [[None] * count for unused in range(count)]
    for outer in range(count):
        for inner in range(outer + 1):
            total = matrix[outer, inner]
            for other in range(inner):
                total = total - lower[outer][other] * lower[inner][other]
            if outer == inner:
                lower[outer][outer] = jnp.sqrt(total)
            else:
                lower[outer][inner] = total / lower[inner][inner]
    solved = []
    for outer in range(count):
        total = target[outer]
        for other in range(outer):
            total = total - lower[outer][other] * solved[other]
        solved.append(total / lower[outer][outer])
    result = [None] * count
    for outer in reversed(range(count)):
        total = solved[outer]
        for other in range(outer + 1, count):
            total = total - lower[other][outer] * result[other]
        result[outer] = total / lower[outer][outer]
    return jnp.stack(result)

def cycle_weights(gram_matrix):
    combined = CENTER * gram_matrix[:-1] + RADIUS * gram_matrix[1:]
    normal_matrix = CENTER * combined[:, :-1] + RADIUS * combined[:, 1:]
    return small_solve(normal_matrix, combined[:, 0])

def residual_weights(weights):
    padding = jnp.zeros((1,) + weights.shape[1:], weights.dtype)
    image = CENTER * jnp.concatenate([weights, padding], 0) + RADIUS * jnp.concatenate([padding, weights], 0)
    first = jnp.zeros_like(image).at[0].set(1.0)
    return first - image

def reference(right_side, blocks, block_cols, send_lists):
    columns = right_side.shape[1]
    shaped_blocks = blocks.reshape(N_SUB, NB_DEV, K, BS, BS)
    shaped_cols = block_cols.reshape(N_SUB, NB_DEV, K)
    list_pad = jnp.zeros((1, 2, HALO), jnp.int32)
    padded_lists = jnp.concatenate([list_pad, send_lists, list_pad], 0)

    def apply_matrix(vector):
        vector_blocks = vector.reshape(N_SUB, NB_DEV, BS, columns)
        padding = jnp.zeros((1, NB_DEV, BS, columns), jnp.float32)
        padded = jnp.concatenate([padding, vector_blocks, padding], 0)

        def device_rows(device):
            left_blocks = padded[device][padded_lists[device, 0]]
            right_blocks = padded[device + 2][padded_lists[device + 2, 1]]
            extended = jnp.concatenate([padded[device + 1], left_blocks, right_blocks], 0)
            total = jnp.zeros((NB_DEV, BS, columns), jnp.float32)
            for slot in range(K):
                total = total + jnp.einsum('bij,bjc->bic', shaped_blocks[device][:, slot], extended[shaped_cols[device][:, slot]], precision=lax.Precision.HIGHEST)
            return total
        return lax.map(device_rows, jnp.arange(N_SUB)).reshape(-1, columns)
    correction = jnp.zeros_like(right_side)
    residual = right_side
    for restart in range(CYCLES):
        krylov = [residual]
        for power in range(STEPS):
            latest = krylov[-1]
            krylov.append((apply_matrix(latest) - CENTER * latest) / RADIUS)
        stacked = jnp.stack(krylov)
        gram_matrix = jnp.einsum('irc,jrc->ijc', stacked, stacked, precision=lax.Precision.HIGHEST)
        weights = cycle_weights(gram_matrix)
        combine = residual_weights(weights)
        update = weights[0][None] * krylov[0]
        for power in range(1, STEPS):
            update = update + weights[power][None] * krylov[power]
        correction = correction + update
        fresh = combine[0][None] * krylov[0]
        for power in range(1, STEPS + 1):
            fresh = fresh + combine[power][None] * krylov[power]
        residual = fresh
    return (correction, residual)
```

```python
import jax
import jax.numpy as jnp
from jax import lax
from jax.experimental import pallas as pl
from jax.experimental.pallas import tpu as pltpu
from jax.sharding import PartitionSpec as P

STEPS = 4
CYCLES = 3
CENTER = 4.5
RADIUS = 3.5
BS = 128
NB = 4
HALO = 2
EXT = NB + 2 * HALO
ROWS = NB * BS
COLS = 32
PAIRS = [(i, j) for i in range(STEPS + 1) for j in range(i, STEPS + 1)]
GROUP = 128 // COLS
GRAM_ROWS = (len(PAIRS) + GROUP - 1) // GROUP

VMEM = pl.BlockSpec(memory_space=pltpu.VMEM)
SMEM = pl.BlockSpec(memory_space=pltpu.SMEM)
PARAMS = pltpu.CompilerParams(vmem_limit_bytes=32 * 1024 * 1024)


def f32(*shape):
    return jax.ShapeDtypeStruct(shape, jnp.float32)


def bf16(*shape):
    return jax.ShapeDtypeStruct(shape, jnp.bfloat16)


def split(value):
    high = value.astype(jnp.bfloat16)
    low = (value - high.astype(jnp.float32)).astype(jnp.bfloat16)
    return high, low


def write_sends(lists, vector, to_next, to_previous):
    for slot in range(HALO):
        for side, target in ((0, to_next), (1, to_previous)):
            start = pl.multiple_of(lists[side, slot] * BS, BS)
            target[:, slot * BS : (slot + 1) * BS] = vector[:, pl.ds(start, BS)]


def operator_kernel(cols, blocks, high, low, dense):
    dense[...] = jnp.zeros_like(dense)
    for row in range(NB):
        for slot in range(blocks.shape[1]):
            start = pl.multiple_of(cols[row, slot] * BS, BS)
            place = (pl.ds(start, BS), slice(row * BS, (row + 1) * BS))
            dense[place] = dense[place] + blocks[row, slot].T
    unit = (
        lax.broadcasted_iota(jnp.int32, (BS, BS), 0) == lax.broadcasted_iota(jnp.int32, (BS, BS), 1)
    ).astype(jnp.float32)
    for row in range(NB):
        for column in range(EXT):
            place = (slice(column * BS, (column + 1) * BS), slice(row * BS, (row + 1) * BS))
            value = dense[place]
            if row == column:
                value = value - CENTER * unit
            high[place], low[place] = split(value * (1.0 / RADIUS))


def start_kernel(lists, core, gathered, vector, to_next, to_previous):
    first = pl.multiple_of(core[0] * COLS, COLS)
    vector[...] = gathered[pl.ds(first, COLS), :]
    write_sends(lists, vector, to_next, to_previous)


def step_kernel(lists, vector, from_previous, from_next, high, low, result, to_next, to_previous):
    extended = jnp.concatenate([vector[...], from_previous[...], from_next[...]], 1)
    top, rest = split(extended)
    first = jnp.dot(
        jnp.concatenate([top, rest], 0), high[...], preferred_element_type=jnp.float32
    )
    second = jnp.dot(top, low[...], preferred_element_type=jnp.float32)
    result[...] = first[:COLS] + (first[COLS:] + second)
    write_sends(lists, result, to_next, to_previous)


def local_gram(vectors, gram):
    products = []
    for i, j in PAIRS:
        total = None
        for tile in range(NB):
            place = slice(tile * BS, (tile + 1) * BS)
            term = vectors[i][:, place] * vectors[j][:, place]
            total = term if total is None else total + term
        products.append(total)
    while len(products) < GRAM_ROWS * GROUP:
        products.append(jnp.zeros((COLS, BS), jnp.float32))
    sums = lax.dot_general(
        jnp.ones((8, BS), jnp.float32),
        jnp.concatenate(products, 0),
        (((1,), (1,)), ((), ())),
        precision=lax.Precision.HIGHEST,
        preferred_element_type=jnp.float32,
    )
    packed = jnp.concatenate([sums[:1, row * BS : (row + 1) * BS] for row in range(GRAM_ROWS)], 0)
    gram[...] = jnp.broadcast_to(packed[None], gram.shape)


def gram_kernel(*refs):
    local_gram([ref[...] for ref in refs[:-1]], refs[-1])


def small_solve(matrix, target):
    count = len(target)
    lower = [[None] * count for unused in range(count)]
    inverse = [None] * count
    for outer in range(count):
        for inner in range(outer + 1):
            total = matrix[outer][inner]
            for other in range(inner):
                total = total - lower[outer][other] * lower[inner][other]
            if outer == inner:
                inverse[outer] = 1.0 / jnp.sqrt(total)
            else:
                lower[outer][inner] = total * inverse[inner]
    solved = []
    for outer in range(count):
        total = target[outer]
        for other in range(outer):
            total = total - lower[outer][other] * solved[other]
        solved.append(total * inverse[outer])
    result = [None] * count
    for outer in reversed(range(count)):
        total = solved[outer]
        for other in range(outer + 1, count):
            total = total - lower[other][outer] * result[other]
        result[outer] = total * inverse[outer]
    return result


def cycle_weights(gathered):
    summed = jnp.sum(gathered, 0)
    padded = jnp.concatenate([summed, jnp.zeros((8 - GRAM_ROWS, BS), jnp.float32)], 0)
    turned = padded.T
    gram = [[None] * (STEPS + 1) for unused in range(STEPS + 1)]
    for index, (i, j) in enumerate(PAIRS):
        first = (index % GROUP) * COLS
        column = turned[first : first + COLS, index // GROUP : index // GROUP + 1]
        gram[i][j] = gram[j][i] = jnp.broadcast_to(column, (COLS, BS))
    combined = [
        [CENTER * gram[i][j] + RADIUS * gram[i + 1][j] for j in range(STEPS + 1)]
        for i in range(STEPS)
    ]
    normal = [
        [CENTER * combined[i][j] + RADIUS * combined[i][j + 1] for j in range(STEPS)]
        for i in range(STEPS)
    ]
    weights = small_solve(normal, [combined[i][0] for i in range(STEPS)])
    left = [1.0 - CENTER * weights[0]]
    for i in range(1, STEPS):
        left.append(-(CENTER * weights[i] + RADIUS * weights[i - 1]))
    left.append(-(RADIUS * weights[STEPS - 1]))
    return weights, left


def combined_tile(weights, vectors, tile):
    place = slice(tile * BS, (tile + 1) * BS)
    total = None
    for weight, vector in zip(weights, vectors):
        term = weight * vector[:, place]
        total = term if total is None else total + term
    return total


def restart_kernel(has_correction, *refs):
    lists, gathered = refs[:2]
    vectors = refs[2 : 2 + 2 * STEPS + 1]
    refs = refs[2 + 2 * STEPS + 1 :]
    if has_correction:
        old, refs = refs[0], refs[1:]
    correction, fresh, gram, to_next, to_previous = refs[0], refs[1:-3], *refs[-3:]
    weights, left = cycle_weights(gathered[...])
    for tile in range(NB):
        place = slice(tile * BS, (tile + 1) * BS)
        update = combined_tile(weights, vectors, tile)
        correction[:, place] = old[:, place] + update if has_correction else update
        for power in range(STEPS + 1):
            fresh[power][:, place] = combined_tile(left, vectors[power:], tile)
    write_sends(lists, fresh[STEPS], to_next, to_previous)
    local_gram([ref[...] for ref in fresh], gram)


def finish_kernel(gathered, *refs):
    vectors = refs[: STEPS + 1]
    old, correction, residual = refs[STEPS + 1 :]
    weights, left = cycle_weights(gathered[...])
    for tile in range(NB):
        place = slice(tile * BS, (tile + 1) * BS)
        correction[:, place] = old[:, place] + combined_tile(weights, vectors, tile)
        residual[:, place] = combined_tile(left, vectors, tile)


def call(kernel, out_shape, smem, vmem, scratch=()):
    return pl.pallas_call(
        kernel,
        out_shape=out_shape,
        in_specs=[SMEM] * len(smem) + [VMEM] * len(vmem),
        out_specs=jax.tree.map(lambda unused: VMEM, out_shape),
        scratch_shapes=scratch,
        compiler_params=PARAMS,
    )(*smem, *vmem)


def on_device(right_side, blocks, block_cols, send_lists):
    subs = lax.axis_size("sub")
    lists = send_lists[0]
    fold = lax.axis_index("fold")
    core = fold % 2
    vector_shape = f32(COLS, ROWS)
    halo_shape = f32(COLS, HALO * BS)
    gram_shape = f32(subs, GRAM_ROWS, BS)
    high, low = call(
        operator_kernel,
        (bf16(EXT * BS, ROWS), bf16(EXT * BS, ROWS)),
        [block_cols],
        [blocks],
        [pltpu.VMEM((EXT * BS, ROWS), jnp.float32)],
    )
    gathered = lax.all_gather(right_side.T, "fold", axis=1, tiled=True)
    vector, to_next, to_previous = call(
        start_kernel,
        (vector_shape, halo_shape, halo_shape),
        [lists, core.astype(jnp.int32).reshape(1)],
        [gathered],
    )

    def passed(value, by):
        return lax.ppermute(value, "sub", [(i, (i + by) % subs) for i in range(subs)])

    def step(vector, to_next, to_previous):
        from_previous = passed(to_next, 1)
        from_next = passed(to_previous, -1)
        return call(
            step_kernel,
            (vector_shape, halo_shape, halo_shape),
            [lists],
            [vector, from_previous, from_next, high, low],
        )

    def exchanged(gram):
        return lax.all_to_all(gram, "sub", 0, 0)

    basis = [vector]
    for power in range(STEPS):
        vector, to_next, to_previous = step(vector, to_next, to_previous)
        basis.append(vector)
    gram = call(gram_kernel, gram_shape, [], basis)
    correction = None
    for restart in range(CYCLES - 1):
        sums = exchanged(gram)
        for power in range(STEPS):
            vector, to_next, to_previous = step(vector, to_next, to_previous)
            basis.append(vector)
        old = [] if correction is None else [correction]
        results = call(
            lambda *refs, held=bool(old): restart_kernel(held, *refs),
            (vector_shape,) * (STEPS + 2) + (gram_shape, halo_shape, halo_shape),
            [lists],
            [sums, *basis, *old],
        )
        correction, basis = results[0], list(results[1 : STEPS + 2])
        gram, to_next, to_previous = results[-3:]
        vector = basis[-1]
    correction, residual = call(
        finish_kernel,
        (vector_shape, vector_shape),
        [],
        [exchanged(gram), *basis, correction],
    )
    both = jnp.stack([correction, residual])
    other = lax.dynamic_slice_in_dim(both, (fold - core + 1 - core) * BS, BS, 2)
    arrived = lax.ppermute(other, "fold", [(0, 1), (1, 0), (2, 3), (3, 2)])
    own = lax.dynamic_slice_in_dim(both, fold * BS, BS, 2)
    whole = jnp.where(
        core == 0, jnp.concatenate([own, arrived], 1), jnp.concatenate([arrived, own], 1)
    )
    return (whole[0].T, whole[1].T)


def solution(mesh):
    placed = (
        P(("sub", "fold"), None),
        P("sub", None, None, None),
        P("sub", None),
        P("sub", None, None),
    )
    return jax.shard_map(
        on_device,
        mesh=mesh,
        in_specs=placed,
        out_specs=(P(("sub", "fold"), None), P(("sub", "fold"), None)),
        check_vma=False,
    )
```

```python
import jax
import jax.numpy as jnp
from jax import lax
from jax.experimental import pallas as pl
from jax.experimental.pallas import tpu as pltpu
from jax.sharding import PartitionSpec as P

STEPS = 4
CYCLES = 3
CENTER = 4.5
RADIUS = 3.5
BS = 128
NB = 4
HALO = 2
EXT = NB + 2 * HALO
ROWS = NB * BS
COLS = 32
PAIRS = [(i, j) for i in range(STEPS + 1) for j in range(i, STEPS + 1)]
GROUP = 128 // COLS
GRAM_ROWS = (len(PAIRS) + GROUP - 1) // GROUP

VMEM = pl.BlockSpec(memory_space=pltpu.VMEM)
SMEM = pl.BlockSpec(memory_space=pltpu.SMEM)
PARAMS = pltpu.CompilerParams(vmem_limit_bytes=32 * 1024 * 1024)


def f32(*shape):
    return jax.ShapeDtypeStruct(shape, jnp.float32)


def bf16(*shape):
    return jax.ShapeDtypeStruct(shape, jnp.bfloat16)


def split(value):
    high = value.astype(jnp.bfloat16)
    value = value - high.astype(jnp.float32)
    middle = value.astype(jnp.bfloat16)
    low = (value - middle.astype(jnp.float32)).astype(jnp.bfloat16)
    return high, middle, low


def product(vector, high, middle, low):
    parts = split(vector)
    first = jnp.dot(
        jnp.concatenate(parts, 0), high[...], preferred_element_type=jnp.float32
    )
    second = jnp.dot(
        jnp.concatenate(parts[:2], 0), middle[...], preferred_element_type=jnp.float32
    )
    third = jnp.dot(parts[0], low[...], preferred_element_type=jnp.float32)
    small = first[2 * COLS :] + second[COLS:] + third
    return first[:COLS] + (first[COLS : 2 * COLS] + second[:COLS] + small)


def write_sends(lists, vector, to_next, to_previous):
    for slot in range(HALO):
        for side, target in ((0, to_next), (1, to_previous)):
            start = pl.multiple_of(lists[side, slot] * BS, BS)
            target[:, slot * BS : (slot + 1) * BS] = vector[:, pl.ds(start, BS)]


def operator_kernel(cols, blocks, *refs):
    own, received, dense = refs[:3], refs[3:6], refs[6]
    dense[...] = jnp.zeros_like(dense)
    for row in range(NB):
        for slot in range(blocks.shape[1]):
            start = pl.multiple_of(cols[row, slot] * BS, BS)
            place = (pl.ds(start, BS), slice(row * BS, (row + 1) * BS))
            dense[place] = dense[place] + blocks[row, slot].T
    unit = (
        lax.broadcasted_iota(jnp.int32, (BS, BS), 0) == lax.broadcasted_iota(jnp.int32, (BS, BS), 1)
    ).astype(jnp.float32)
    for row in range(NB):
        for column in range(EXT):
            place = (slice(column * BS, (column + 1) * BS), slice(row * BS, (row + 1) * BS))
            value = dense[place]
            if row == column:
                value = value - CENTER * unit
            targets = own if column < NB else received
            start = (column % NB) * BS
            for target, part in zip(targets, split(value * (1.0 / RADIUS))):
                target[start : start + BS, row * BS : (row + 1) * BS] = part


def start_kernel(lists, core, gathered, vector, to_next, to_previous):
    first = pl.multiple_of(core[0] * COLS, COLS)
    vector[...] = gathered[pl.ds(first, COLS), :]
    write_sends(lists, vector, to_next, to_previous)


def own_kernel(vector, high, middle, low, partial):
    partial[...] = product(vector[...], high, middle, low)


def step_kernel(lists, partial, from_previous, from_next, *refs):
    parts, (result, to_next, to_previous) = refs[:3], refs[3:]
    received = jnp.concatenate([from_previous[...], from_next[...]], 1)
    result[...] = partial[...] + product(received, *parts)
    write_sends(lists, result, to_next, to_previous)


def local_gram(vectors, gram):
    products = []
    for i, j in PAIRS:
        total = None
        for tile in range(NB):
            place = slice(tile * BS, (tile + 1) * BS)
            term = vectors[i][:, place] * vectors[j][:, place]
            total = term if total is None else total + term
        products.append(total)
    while len(products) < GRAM_ROWS * GROUP:
        products.append(jnp.zeros((COLS, BS), jnp.float32))
    sums = lax.dot_general(
        jnp.ones((8, BS), jnp.float32),
        jnp.concatenate(products, 0),
        (((1,), (1,)), ((), ())),
        precision=lax.Precision.HIGHEST,
        preferred_element_type=jnp.float32,
    )
    packed = jnp.concatenate([sums[:1, row * BS : (row + 1) * BS] for row in range(GRAM_ROWS)], 0)
    gram[...] = jnp.broadcast_to(packed[None], gram.shape)


def gram_kernel(*refs):
    local_gram([ref[...] for ref in refs[:-1]], refs[-1])


def small_solve(matrix, target):
    count = len(target)
    lower = [[None] * count for unused in range(count)]
    inverse = [None] * count
    for outer in range(count):
        for inner in range(outer + 1):
            total = matrix[outer][inner]
            for other in range(inner):
                total = total - lower[outer][other] * lower[inner][other]
            if outer == inner:
                inverse[outer] = 1.0 / jnp.sqrt(total)
            else:
                lower[outer][inner] = total * inverse[inner]
    solved = []
    for outer in range(count):
        total = target[outer]
        for other in range(outer):
            total = total - lower[outer][other] * solved[other]
        solved.append(total * inverse[outer])
    result = [None] * count
    for outer in reversed(range(count)):
        total = solved[outer]
        for other in range(outer + 1, count):
            total = total - lower[other][outer] * result[other]
        result[outer] = total * inverse[outer]
    return result


def cycle_weights(gathered):
    summed = jnp.sum(gathered, 0)
    padded = jnp.concatenate([summed, jnp.zeros((8 - GRAM_ROWS, BS), jnp.float32)], 0)
    turned = padded.T
    gram = [[None] * (STEPS + 1) for unused in range(STEPS + 1)]
    for index, (i, j) in enumerate(PAIRS):
        first = (index % GROUP) * COLS
        column = turned[first : first + COLS, index // GROUP : index // GROUP + 1]
        gram[i][j] = gram[j][i] = jnp.broadcast_to(column, (COLS, BS))
    combined = [
        [CENTER * gram[i][j] + RADIUS * gram[i + 1][j] for j in range(STEPS + 1)]
        for i in range(STEPS)
    ]
    normal = [
        [CENTER * combined[i][j] + RADIUS * combined[i][j + 1] for j in range(STEPS)]
        for i in range(STEPS)
    ]
    weights = small_solve(normal, [combined[i][0] for i in range(STEPS)])
    left = [1.0 - CENTER * weights[0]]
    for i in range(1, STEPS):
        left.append(-(CENTER * weights[i] + RADIUS * weights[i - 1]))
    left.append(-(RADIUS * weights[STEPS - 1]))
    return weights, left


def combined_tile(weights, vectors, tile):
    place = slice(tile * BS, (tile + 1) * BS)
    total = None
    for weight, vector in zip(weights, vectors):
        term = weight * vector[:, place]
        total = term if total is None else total + term
    return total


def restart_kernel(has_correction, *refs):
    lists, gathered = refs[:2]
    vectors = refs[2 : 2 + 2 * STEPS + 1]
    refs = refs[2 + 2 * STEPS + 1 :]
    if has_correction:
        old, refs = refs[0], refs[1:]
    correction, fresh, gram, to_next, to_previous = refs[0], refs[1:-3], *refs[-3:]
    weights, left = cycle_weights(gathered[...])
    for tile in range(NB):
        place = slice(tile * BS, (tile + 1) * BS)
        update = combined_tile(weights, vectors, tile)
        correction[:, place] = old[:, place] + update if has_correction else update
        for power in range(STEPS + 1):
            fresh[power][:, place] = combined_tile(left, vectors[power:], tile)
    write_sends(lists, fresh[STEPS], to_next, to_previous)
    local_gram([ref[...] for ref in fresh], gram)


def finish_kernel(gathered, *refs):
    vectors = refs[: STEPS + 1]
    old, correction, residual = refs[STEPS + 1 :]
    weights, left = cycle_weights(gathered[...])
    for tile in range(NB):
        place = slice(tile * BS, (tile + 1) * BS)
        correction[:, place] = old[:, place] + combined_tile(weights, vectors, tile)
        residual[:, place] = combined_tile(left, vectors, tile)


def call(kernel, out_shape, smem, vmem, scratch=(), flops=10**6):
    return pl.pallas_call(
        kernel,
        out_shape=out_shape,
        in_specs=[SMEM] * len(smem) + [VMEM] * len(vmem),
        out_specs=jax.tree.map(lambda unused: VMEM, out_shape),
        scratch_shapes=scratch,
        compiler_params=PARAMS,
        cost_estimate=pl.CostEstimate(flops=flops, bytes_accessed=2**20, transcendentals=0),
    )(*smem, *vmem)


def on_device(right_side, blocks, block_cols, send_lists):
    subs = lax.axis_size("sub")
    lists = send_lists[0]
    fold = lax.axis_index("fold")
    core = fold % 2
    vector_shape = f32(COLS, ROWS)
    halo_shape = f32(COLS, HALO * BS)
    gram_shape = f32(subs, GRAM_ROWS, BS)
    operator = call(
        operator_kernel,
        (bf16(ROWS, ROWS),) * 6,
        [block_cols],
        [blocks],
        [pltpu.VMEM((EXT * BS, ROWS), jnp.float32)],
    )
    gathered = lax.all_gather(right_side.T, "fold", axis=1, tiled=True)
    vector, to_next, to_previous = call(
        start_kernel,
        (vector_shape, halo_shape, halo_shape),
        [lists, core.astype(jnp.int32).reshape(1)],
        [gathered],
    )

    def passed(value, by):
        return lax.ppermute(value, "sub", [(i, (i + by) % subs) for i in range(subs)])

    def step(vector, to_next, to_previous):
        from_previous = passed(to_next, 1)
        from_next = passed(to_previous, -1)
        partial = call(own_kernel, vector_shape, [], [vector, *operator[:3]], flops=10**9)
        return call(
            step_kernel,
            (vector_shape, halo_shape, halo_shape),
            [lists],
            [partial, from_previous, from_next, *operator[3:]],
        )

    def exchanged(gram):
        return lax.all_to_all(gram, "sub", 0, 0)

    basis = [vector]
    for power in range(STEPS):
        vector, to_next, to_previous = step(vector, to_next, to_previous)
        basis.append(vector)
    gram = call(gram_kernel, gram_shape, [], basis)
    correction = None
    for restart in range(CYCLES - 1):
        sums = exchanged(gram)
        for power in range(STEPS):
            vector, to_next, to_previous = step(vector, to_next, to_previous)
            basis.append(vector)
        old = [] if correction is None else [correction]
        results = call(
            lambda *refs, held=bool(old): restart_kernel(held, *refs),
            (vector_shape,) * (STEPS + 2) + (gram_shape, halo_shape, halo_shape),
            [lists],
            [sums, *basis, *old],
        )
        correction, basis = results[0], list(results[1 : STEPS + 2])
        gram, to_next, to_previous = results[-3:]
        vector = basis[-1]
    correction, residual = call(
        finish_kernel,
        (vector_shape, vector_shape),
        [],
        [exchanged(gram), *basis, correction],
    )
    both = jnp.stack([correction, residual])
    other = lax.dynamic_slice_in_dim(both, (fold - core + 1 - core) * BS, BS, 2)
    arrived = lax.ppermute(other, "fold", [(0, 1), (1, 0), (2, 3), (3, 2)])
    own = lax.dynamic_slice_in_dim(both, fold * BS, BS, 2)
    whole = jnp.where(
        core == 0, jnp.concatenate([own, arrived], 1), jnp.concatenate([arrived, own], 1)
    )
    return (whole[0].T, whole[1].T)


def solution(mesh):
    placed = (
        P(("sub", "fold"), None),
        P("sub", None, None, None),
        P("sub", None),
        P("sub", None, None),
    )
    return jax.shard_map(
        on_device,
        mesh=mesh,
        in_specs=placed,
        out_specs=(P(("sub", "fold"), None), P(("sub", "fold"), None)),
        check_vma=False,
    )
```

```python
import functools

import jax
import jax.numpy as jnp
from jax import lax
from jax.experimental import pallas as pl
from jax.experimental.pallas import tpu as pltpu
from jax.sharding import PartitionSpec as P

STEPS = 4
CYCLES = 3
CENTER = 4.5
RADIUS = 3.5
BS = 128
NB = 4
HALO = 2
EXT = NB + 2 * HALO
ROWS = NB * BS
COLS = 32
PAIRS = [(i, j) for i in range(STEPS + 1) for j in range(i, STEPS + 1)]
GROUP = 128 // COLS
GRAM_ROWS = (len(PAIRS) + GROUP - 1) // GROUP

COUNT = STEPS * CYCLES + 1
SUBLANES = 8
PART = 8
TILES = -(-COUNT * (COUNT + 1) // 2 // (SUBLANES * GROUP))
SUM_ROWS = TILES * SUBLANES
LIMIT = 2000.0

VMEM = pl.BlockSpec(memory_space=pltpu.VMEM)
SMEM = pl.BlockSpec(memory_space=pltpu.SMEM)
PARAMS = pltpu.CompilerParams(vmem_limit_bytes=32 * 1024 * 1024)


def f32(*shape):
    return jax.ShapeDtypeStruct(shape, jnp.float32)


def bf16(*shape):
    return jax.ShapeDtypeStruct(shape, jnp.bfloat16)


def split(value):
    high = value.astype(jnp.bfloat16)
    value = value - high.astype(jnp.float32)
    middle = value.astype(jnp.bfloat16)
    low = (value - middle.astype(jnp.float32)).astype(jnp.bfloat16)
    return high, middle, low


def product(vector, high, middle, low):
    parts = split(vector)
    first = jnp.dot(
        jnp.concatenate(parts, 0), high[...], preferred_element_type=jnp.float32
    )
    second = jnp.dot(
        jnp.concatenate(parts[:2], 0), middle[...], preferred_element_type=jnp.float32
    )
    third = jnp.dot(parts[0], low[...], preferred_element_type=jnp.float32)
    small = first[2 * COLS :] + second[COLS:] + third
    return first[:COLS] + (first[COLS : 2 * COLS] + second[:COLS] + small)


def write_sends(lists, vector, to_next, to_previous):
    for slot in range(HALO):
        for side, target in ((0, to_next), (1, to_previous)):
            start = pl.multiple_of(lists[side, slot] * BS, BS)
            target[:, slot * BS : (slot + 1) * BS] = vector[:, pl.ds(start, BS)]


def operator_kernel(cols, lists, blocks, *refs):
    own, received, masks, dense = refs[:3], refs[3:6], refs[6], refs[7]
    for side in range(2):
        for slot in range(HALO):
            for block in range(NB):
                chosen = jnp.full((SUBLANES, BS), lists[side, slot], jnp.int32) == block
                masks[side * HALO + slot, block] = jnp.where(chosen, 1.0, 0.0)
    dense[...] = jnp.zeros_like(dense)
    for row in range(NB):
        for slot in range(blocks.shape[1]):
            start = pl.multiple_of(cols[row, slot] * BS, BS)
            place = (pl.ds(start, BS), slice(row * BS, (row + 1) * BS))
            dense[place] = dense[place] + blocks[row, slot].T
    unit = (
        lax.broadcasted_iota(jnp.int32, (BS, BS), 0) == lax.broadcasted_iota(jnp.int32, (BS, BS), 1)
    ).astype(jnp.float32)
    for row in range(NB):
        for column in range(EXT):
            place = (slice(column * BS, (column + 1) * BS), slice(row * BS, (row + 1) * BS))
            value = dense[place]
            if row == column:
                value = value - CENTER * unit
            targets = own if column < NB else received
            start = (column % NB) * BS
            for target, part in zip(targets, split(value * (1.0 / RADIUS))):
                target[start : start + BS, row * BS : (row + 1) * BS] = part


def write_chosen(masks, vector, to_next, to_previous):
    repeats = vector.shape[0] // SUBLANES
    for slot in range(HALO):
        for side, target in ((0, to_next), (1, to_previous)):
            total = None
            for block in range(NB):
                mask = jnp.concatenate([masks[side * HALO + slot, block]] * repeats, 0)
                value = vector[:, block * BS : (block + 1) * BS]
                total = value if total is None else jnp.where(mask > 0.5, value, total)
            target[:, slot * BS : (slot + 1) * BS] = total


def start_kernel(lists, core, gathered, vector, to_next, to_previous):
    first = pl.multiple_of(core[0] * COLS, COLS)
    vector[...] = gathered[pl.ds(first, COLS), :]
    write_sends(lists, vector, to_next, to_previous)


def own_kernel(vector, high, middle, low, partial):
    partial[...] = product(vector[...], high, middle, low)


def step_kernel(masks, partial, from_previous, from_next, *refs):
    parts, (result, to_next, to_previous) = refs[:3], refs[3:]
    received = jnp.concatenate([from_previous[...], from_next[...]], 1)
    vector = partial[...] + product(received, *parts)
    result[...] = vector
    write_chosen(masks, vector, to_next, to_previous)


def local_gram(vectors, gram):
    products = []
    for i, j in PAIRS:
        total = None
        for tile in range(NB):
            place = slice(tile * BS, (tile + 1) * BS)
            term = vectors[i][:, place] * vectors[j][:, place]
            total = term if total is None else total + term
        products.append(total)
    while len(products) < GRAM_ROWS * GROUP:
        products.append(jnp.zeros((COLS, BS), jnp.float32))
    sums = lax.dot_general(
        jnp.ones((8, BS), jnp.float32),
        jnp.concatenate(products, 0),
        (((1,), (1,)), ((), ())),
        precision=lax.Precision.HIGHEST,
        preferred_element_type=jnp.float32,
    )
    packed = jnp.concatenate([sums[:1, row * BS : (row + 1) * BS] for row in range(GRAM_ROWS)], 0)
    gram[...] = jnp.broadcast_to(packed[None], gram.shape)


def gram_kernel(*refs):
    local_gram([ref[...] for ref in refs[:-1]], refs[-1])


def small_solve(matrix, target):
    count = len(target)
    lower = [[None] * count for unused in range(count)]
    inverse = [None] * count
    for outer in range(count):
        for inner in range(outer + 1):
            total = matrix[outer][inner]
            for other in range(inner):
                total = total - lower[outer][other] * lower[inner][other]
            if outer == inner:
                inverse[outer] = 1.0 / jnp.sqrt(total)
            else:
                lower[outer][inner] = total * inverse[inner]
    solved = []
    for outer in range(count):
        total = target[outer]
        for other in range(outer):
            total = total - lower[outer][other] * solved[other]
        solved.append(total * inverse[outer])
    result = [None] * count
    for outer in reversed(range(count)):
        total = solved[outer]
        for other in range(outer + 1, count):
            total = total - lower[other][outer] * result[other]
        result[outer] = total * inverse[outer]
    return result


def cycle_weights(gathered):
    summed = jnp.sum(gathered, 0)
    padded = jnp.concatenate([summed, jnp.zeros((8 - GRAM_ROWS, BS), jnp.float32)], 0)
    turned = padded.T
    gram = [[None] * (STEPS + 1) for unused in range(STEPS + 1)]
    for index, (i, j) in enumerate(PAIRS):
        first = (index % GROUP) * COLS
        column = turned[first : first + COLS, index // GROUP : index // GROUP + 1]
        gram[i][j] = gram[j][i] = jnp.broadcast_to(column, (COLS, BS))
    combined = [
        [CENTER * gram[i][j] + RADIUS * gram[i + 1][j] for j in range(STEPS + 1)]
        for i in range(STEPS)
    ]
    normal = [
        [CENTER * combined[i][j] + RADIUS * combined[i][j + 1] for j in range(STEPS)]
        for i in range(STEPS)
    ]
    weights = small_solve(normal, [combined[i][0] for i in range(STEPS)])
    left = [1.0 - CENTER * weights[0]]
    for i in range(1, STEPS):
        left.append(-(CENTER * weights[i] + RADIUS * weights[i - 1]))
    left.append(-(RADIUS * weights[STEPS - 1]))
    return weights, left


def combined_tile(weights, vectors, tile):
    place = slice(tile * BS, (tile + 1) * BS)
    total = None
    for weight, vector in zip(weights, vectors):
        term = weight * vector[:, place]
        total = term if total is None else total + term
    return total


def restart_kernel(has_correction, *refs):
    lists, gathered = refs[:2]
    vectors = refs[2 : 2 + 2 * STEPS + 1]
    refs = refs[2 + 2 * STEPS + 1 :]
    if has_correction:
        old, refs = refs[0], refs[1:]
    correction, fresh, gram, to_next, to_previous = refs[0], refs[1:-3], *refs[-3:]
    weights, left = cycle_weights(gathered[...])
    for tile in range(NB):
        place = slice(tile * BS, (tile + 1) * BS)
        update = combined_tile(weights, vectors, tile)
        correction[:, place] = old[:, place] + update if has_correction else update
        for power in range(STEPS + 1):
            fresh[power][:, place] = combined_tile(left, vectors[power:], tile)
    write_sends(lists, fresh[STEPS], to_next, to_previous)
    local_gram([ref[...] for ref in fresh], gram)


def finish_kernel(gathered, *refs):
    vectors = refs[: STEPS + 1]
    old, correction, residual = refs[STEPS + 1 :]
    weights, left = cycle_weights(gathered[...])
    for tile in range(NB):
        place = slice(tile * BS, (tile + 1) * BS)
        correction[:, place] = old[:, place] + combined_tile(weights, vectors, tile)
        residual[:, place] = combined_tile(left, vectors, tile)


def two_sum(left, right):
    total = left + right
    shadow = total - left
    return total, (left - (total - shadow)) + (right - shadow)


def coarse_split(value):
    grid = jnp.max(jnp.abs(value), 0, keepdims=True) * (1.5 * 2.0**15)
    coarse = (value + grid) - grid
    return coarse, value - coarse


def gram_row(vector, earlier):
    turned = jnp.concatenate([vector[:, i * BS : (i + 1) * BS] for i in range(NB)], 0).T
    coarse, rest = coarse_split(turned)
    row = []
    for other, other_rest in [*earlier, (coarse, rest)]:
        high = low = None
        for start in range(0, BS, SUBLANES):
            place = slice(start, start + SUBLANES)
            main = other[place] * coarse[place]
            side = other[place] * rest[place] + other_rest[place] * turned[place]
            high = main if high is None else high + main
            low = side if low is None else low + side
        row.append((high, low))
    return coarse, rest, row


def round_kernel(*refs):
    vector, parts, earlier = refs[0], refs[1:4], refs[4:-5]
    partial, coarse, rest, high, low = refs[-5:]
    value = vector[...]
    partial[...] = product(value, *parts)
    earlier = [(earlier[i], earlier[i + 1]) for i in range(0, len(earlier), 2)]
    coarse[...], rest[...], row = gram_row(value, earlier)
    for index, (one, other) in enumerate(row):
        high[index], low[index] = one, other


def pack_kernel(*refs):
    vector, earlier = refs[0], refs[1 : 1 + 2 * (COUNT - 1)]
    sums, packed = refs[1 + 2 * (COUNT - 1) : -1], refs[-1]
    earlier = [(earlier[i], earlier[i + 1]) for i in range(0, len(earlier), 2)]
    pairs = []
    for index in range(0, len(sums), 2):
        for i in range(sums[index].shape[0]):
            pairs.append((sums[index][i], sums[index + 1][i]))
    pairs += gram_row(vector[...], earlier)[2]
    sublane = lax.broadcasted_iota(jnp.int32, (SUBLANES, BS), 0)
    lane = lax.broadcasted_iota(jnp.int32, (SUBLANES, BS), 1) // COLS

    def folded(high, low, shift, axis):
        high, error = two_sum(high, pltpu.roll(high, shift, axis))
        return high, low + pltpu.roll(low, shift, axis) + error

    zero = jnp.zeros((SUBLANES, BS), jnp.float32)
    for tile in range(TILES):
        tile_high, tile_low = zero, zero
        for group in range(GROUP):
            high, low = zero, zero
            for row in range(SUBLANES):
                index = (tile * GROUP + group) * SUBLANES + row
                if index < len(pairs):
                    one, other = pairs[index]
                    for shift in (4, 2, 1):
                        one, other = folded(one, other, shift, 0)
                    high = jnp.where(sublane == row, one, high)
                    low = jnp.where(sublane == row, other, low)
            for shift in (2 * COLS, COLS):
                high, low = folded(high, low, shift, 1)
            tile_high = jnp.where(lane == group, high, tile_high)
            tile_low = jnp.where(lane == group, low, tile_low)
        tile_high, tile_low = two_sum(tile_high, tile_low)
        for copy in range(PART):
            packed[copy, tile * SUBLANES : (tile + 1) * SUBLANES] = tile_high
            packed[copy, SUM_ROWS + tile * SUBLANES : SUM_ROWS + (tile + 1) * SUBLANES] = tile_low


def summed(parts):
    high, low = parts[0, :SUM_ROWS], parts[0, SUM_ROWS:]
    for index in range(1, PART):
        high, error = two_sum(high, parts[index, :SUM_ROWS])
        low = low + parts[index, SUM_ROWS:] + error
    return two_sum(high, low)


def sum_kernel(parts, total):
    high, low = summed(parts)
    for copy in range(PART):
        total[copy, :SUM_ROWS] = high
        total[copy, SUM_ROWS:] = low


def halves(value):
    scaled = value * 4097.0
    high = scaled - (scaled - value)
    return high, value - high


def added_product(total, factor, value):
    factor, factor_high, factor_low = factor
    value, low, value_high, value_low = value
    main = factor_high * value_high
    side = factor_high * value_low + (factor_low * value + factor * low)
    if total is None:
        return main, side
    high, error = two_sum(total[0], main)
    return high, total[1] + (error + side)


def basis_gram(coefficients, gram):
    depth = gram[0][0].shape[0]
    index = lax.broadcasted_iota(jnp.int32, (depth, BS), 0)
    wide = [jnp.concatenate([value] * (depth // SUBLANES), 0) for value in coefficients]
    factors = [(value, *halves(value)) for value in wide]
    rows = []
    for i in range(STEPS + 1):
        total = None
        for a, factor in enumerate(factors):
            total = added_product(total, factor, gram[a + i])
        high, low = two_sum(*total)
        rows.append((high, low, *halves(high)))
    result = [[None] * (STEPS + 1) for unused in range(STEPS + 1)]
    for j in range(STEPS + 1):
        shifted = jnp.zeros((depth, BS), jnp.float32)
        for a, value in enumerate(wide):
            shifted = jnp.where(index == a + j, value, shifted)
        factor = (shifted, *halves(shifted))
        for i in range(j + 1):
            high, low = added_product(None, factor, rows[i])
            size = depth
            while size > SUBLANES:
                size //= 2
                high, error = two_sum(high[:size], high[size:])
                low = low[:size] + low[size:] + error
            for shift in (4, 2, 1):
                high, error = two_sum(high, pltpu.roll(high, shift, 0))
                low = low + pltpu.roll(low, shift, 0) + error
            result[i][j] = result[j][i] = high + low
    return result


def solved_weights(gram):
    combined = [
        [CENTER * gram[i][j] + RADIUS * gram[i + 1][j] for j in range(STEPS + 1)]
        for i in range(STEPS)
    ]
    normal = [
        [CENTER * combined[i][j] + RADIUS * combined[i][j + 1] for j in range(STEPS)]
        for i in range(STEPS)
    ]
    weights = small_solve(normal, [combined[i][0] for i in range(STEPS)])
    left = [1.0 - CENTER * weights[0]]
    for i in range(1, STEPS):
        left.append(-(CENTER * weights[i] + RADIUS * weights[i - 1]))
    left.append(-(RADIUS * weights[STEPS - 1]))
    return weights, left


def convolved(left, right):
    result = [None] * (len(left) + len(right) - 1)
    for i, one in enumerate(left):
        for j, other in enumerate(right):
            term = one * other
            result[i + j] = term if result[i + j] is None else result[i + j] + term
    return result


def all_cycles_kernel(fold, parts, *refs):
    vectors, own, other = refs[:COUNT], refs[COUNT], refs[COUNT + 1]
    high, low = summed(parts)
    rolled = [(high, low)]
    for group in range(1, GROUP):
        shift = BS - group * COLS
        rolled.append((pltpu.roll(high, shift, 1), pltpu.roll(low, shift, 1)))

    def entry(i, j):
        index = max(i, j) * (max(i, j) + 1) // 2 + min(i, j)
        tile, rest = divmod(index, SUBLANES * GROUP)
        group, row = divmod(rest, SUBLANES)
        row += tile * SUBLANES
        return [value[row : row + 1] for value in rolled[group]]

    depth = 2 * SUBLANES
    padding = [jnp.zeros((depth - COUNT, BS), jnp.float32)]
    gram = []
    for i in range(COUNT):
        entries = [entry(i, j) for j in range(COUNT)]
        value = jnp.concatenate([one for one, unused in entries] + padding, 0)
        rest = jnp.concatenate([one for unused, one in entries] + padding, 0)
        gram.append((value, rest, *halves(value)))

    def spread(value):
        return jnp.broadcast_to(value, (SUBLANES, BS))

    here = [[spread(entry(i, j)[0]) for j in range(STEPS + 1)] for i in range(STEPS + 1)]
    weights, polynomial = solved_weights(here)
    solution_part = list(weights)
    for cycle in range(1, CYCLES):
        here = basis_gram(polynomial, gram)
        weights, left = solved_weights(here)
        update = convolved(polynomial, weights)
        solution_part = [
            one + solution_part[i] if i < len(solution_part) else one
            for i, one in enumerate(update)
        ]
        polynomial = convolved(polynomial, left)
    remaining = None
    for i in range(STEPS + 1):
        for j in range(STEPS + 1):
            term = (left[i] * left[j]) * here[i][j]
            remaining = term if remaining is None else remaining + term
    reach = None
    for i in range(COUNT):
        term = jnp.abs(polynomial[i]) * jnp.sqrt(spread(entry(i, i)[0]))
        reach = term if reach is None else reach + term
    lane = lax.broadcasted_iota(jnp.int32, (SUBLANES, BS), 1)
    fine = (reach < LIMIT * jnp.sqrt(remaining)) | (lane >= COLS)
    bad = jnp.max(jnp.where(fine, 0.0, 1.0), axis=(0, 1), keepdims=True)
    other[2 * COLS :] = jnp.broadcast_to(bad, (SUBLANES, BS))
    index = lax.broadcasted_iota(jnp.int32, (depth, BS), 0)
    stacked = []
    for values in (solution_part, polynomial):
        total = jnp.zeros((depth, BS), jnp.float32)
        for i, value in enumerate(values):
            value = jnp.concatenate([value] * (depth // SUBLANES), 0)
            total = jnp.where(index == i, value, total)
        stacked.append(total)
    turned = jnp.concatenate(stacked, 0).T
    place = fold[0]
    partner = place + 1 - 2 * (place % 2)
    for output in range(2):
        sums = [None, None]
        for i in range(COUNT - 1 + output):
            column = output * depth + i
            weight = jnp.broadcast_to(turned[:COLS, column : column + 1], (COLS, BS))
            for side, block in enumerate((place, partner)):
                value = vectors[i][:, pl.ds(pl.multiple_of(block * BS, BS), BS)]
                term = weight * value
                sums[side] = term if sums[side] is None else sums[side] + term
        own[output * COLS : (output + 1) * COLS] = sums[0]
        other[output * COLS : (output + 1) * COLS] = sums[1]


def call(kernel, out_shape, smem, vmem, scratch=(), flops=10**6):
    return pl.pallas_call(
        kernel,
        out_shape=out_shape,
        in_specs=[SMEM] * len(smem) + [VMEM] * len(vmem),
        out_specs=jax.tree.map(lambda unused: VMEM, out_shape),
        scratch_shapes=scratch,
        compiler_params=PARAMS,
        cost_estimate=pl.CostEstimate(flops=flops, bytes_accessed=2**20, transcendentals=0),
    )(*smem, *vmem)


def exchanged_over(groups):
    def exchanged(value):
        return lax.all_to_all(value, "sub", 0, 0, axis_index_groups=groups)

    return exchanged


def passed(value, by):
    subs = lax.axis_size("sub")
    return lax.ppermute(value, "sub", [(i, (i + by) % subs) for i in range(subs)])


def swapped(value):
    return lax.ppermute(value, "fold", [(0, 1), (1, 0), (2, 3), (3, 2)])


VECTOR = f32(COLS, ROWS)
HALO_PART = f32(COLS, HALO * BS)


def prepared(gathered, blocks, block_cols, lists, core):
    results = call(
        operator_kernel,
        (bf16(ROWS, ROWS),) * 6 + (f32(2 * HALO, NB, SUBLANES, BS),),
        [block_cols, lists],
        [blocks],
        [pltpu.VMEM((EXT * BS, ROWS), jnp.float32)],
    )
    sends = call(
        start_kernel,
        (VECTOR, HALO_PART, HALO_PART),
        [lists, core],
        [gathered],
    )
    return results[:3], results[3:6], results[6], sends


def stepped(partial, to_next, to_previous, masks, operator):
    return call(
        step_kernel,
        (VECTOR, HALO_PART, HALO_PART),
        [],
        [masks, partial, passed(to_next, 1), passed(to_previous, -1), *operator],
    )


def joined(own, arrived, core):
    both = jnp.concatenate([own[:, None], arrived[:, None]], 1)
    both = jnp.where(core == 0, both, both[:, ::-1])
    whole = both.reshape(2, 2 * COLS, BS)
    return (whole[0].T, whole[1].T)


def cycle_by_cycle(gathered, blocks, block_cols, lists, fold, core):
    gram_shape = f32(lax.axis_size("sub"), GRAM_ROWS, BS)
    operator, received, masks, sends = prepared(gathered, blocks, block_cols, lists, core)

    def step(vector, to_next, to_previous):
        partial = call(own_kernel, VECTOR, [], [vector, *operator], flops=10**9)
        return stepped(partial, to_next, to_previous, masks, received)

    def exchanged(gram):
        return lax.all_to_all(gram, "sub", 0, 0)

    basis = [sends[0]]
    for power in range(STEPS):
        sends = step(*sends)
        basis.append(sends[0])
    gram = call(gram_kernel, gram_shape, [], basis)
    correction = None
    for restart in range(CYCLES - 1):
        sums = exchanged(gram)
        for power in range(STEPS):
            sends = step(*sends)
            basis.append(sends[0])
        old = [] if correction is None else [correction]
        results = call(
            functools.partial(restart_kernel, bool(old)),
            (VECTOR,) * (STEPS + 2) + (gram_shape, HALO_PART, HALO_PART),
            [lists],
            [sums, *basis, *old],
        )
        correction, basis = results[0], list(results[1 : STEPS + 2])
        gram = results[-3]
        sends = (basis[-1], *results[-2:])
    both = call(
        finish_kernel,
        (VECTOR, VECTOR),
        [],
        [exchanged(gram), *basis, correction],
    )
    both = jnp.stack(both)
    partner = fold + 1 - 2 * (fold % 2)
    arrived = swapped(lax.dynamic_slice_in_dim(both, partner * BS, BS, 2))
    own = lax.dynamic_slice_in_dim(both, fold * BS, BS, 2)
    return joined(own, arrived, core[0])


def on_device(right_side, blocks, block_cols, send_lists):
    subs = lax.axis_size("sub")
    lists = send_lists[0]
    fold = lax.axis_index("fold").astype(jnp.int32)
    core = (fold % 2).reshape(1)
    gathered = lax.all_gather(right_side.T, "fold", axis=1, tiled=True)
    operator, received, masks, sends = prepared(gathered, blocks, block_cols, lists, core)
    square = f32(BS, BS)
    vectors, earlier, sums = [sends[0]], [], []
    for power in range(COUNT - 1):
        row = f32(power + 1, SUBLANES, BS)
        partial, coarse, rest, high, low = call(
            round_kernel,
            (VECTOR, square, square, row, row),
            [],
            [sends[0], *operator, *earlier],
            flops=10**9,
        )
        earlier += [coarse, rest]
        sums += [high, low]
        sends = stepped(partial, *sends[1:], masks, received)
        vectors.append(sends[0])
    packed = f32(PART, 2 * SUM_ROWS, BS)
    sums = call(pack_kernel, packed, [], [vectors[-1], *earlier, *sums])
    strided = [[i + PART * j for j in range(subs // PART)] for i in range(PART)]
    runs = [[PART * i + j for j in range(PART)] for i in range(subs // PART)]
    sums = call(sum_kernel, packed, [], [exchanged_over(strided)(sums)])
    own, other = call(
        all_cycles_kernel,
        (f32(2 * COLS, BS), f32(2 * COLS + SUBLANES, BS)),
        [fold.reshape(1)],
        [exchanged_over(runs)(sums), *vectors],
    )
    arrived = swapped(other)
    bad = jnp.maximum(other[2 * COLS, 0], arrived[2 * COLS, 0]) > 0.5
    shape = (2, COLS, BS)
    return lax.cond(
        bad,
        lambda own, arrived, *rest: cycle_by_cycle(*rest),
        lambda own, arrived, *rest: joined(own.reshape(shape), arrived.reshape(shape), core[0]),
        own,
        arrived[: 2 * COLS],
        gathered,
        blocks,
        block_cols,
        lists,
        fold,
        core,
    )


def solution(mesh):
    placed = (
        P(("sub", "fold"), None),
        P("sub", None, None, None),
        P("sub", None),
        P("sub", None, None),
    )
    return jax.shard_map(
        on_device,
        mesh=mesh,
        in_specs=placed,
        out_specs=(P(("sub", "fold"), None), P(("sub", "fold"), None)),
        check_vma=False,
    )
```

```python
import functools

import jax
import jax.numpy as jnp
from jax import lax
from jax.experimental import pallas as pl
from jax.experimental.pallas import tpu as pltpu
from jax.sharding import PartitionSpec as P

STEPS = 4
CYCLES = 3
CENTER = 4.5
RADIUS = 3.5
BS = 128
NB = 4
HALO = 2
EXT = NB + 2 * HALO
ROWS = NB * BS
COLS = 32
PAIRS = [(i, j) for i in range(STEPS + 1) for j in range(i, STEPS + 1)]
GROUP = 128 // COLS
GRAM_ROWS = (len(PAIRS) + GROUP - 1) // GROUP

COUNT = STEPS * CYCLES + 1
SUBLANES = 8
PART = 8
TILES = -(-COUNT * (COUNT + 1) // 2 // (SUBLANES * GROUP))
SUM_ROWS = TILES * SUBLANES
LIMIT = 2000.0

VMEM = pl.BlockSpec(memory_space=pltpu.VMEM)
SMEM = pl.BlockSpec(memory_space=pltpu.SMEM)
PARAMS = pltpu.CompilerParams(vmem_limit_bytes=32 * 1024 * 1024)


def f32(*shape):
    return jax.ShapeDtypeStruct(shape, jnp.float32)


def bf16(*shape):
    return jax.ShapeDtypeStruct(shape, jnp.bfloat16)


def split(value):
    high = value.astype(jnp.bfloat16)
    value = value - high.astype(jnp.float32)
    middle = value.astype(jnp.bfloat16)
    low = (value - middle.astype(jnp.float32)).astype(jnp.bfloat16)
    return high, middle, low


def product(vector, high, middle, low):
    parts = split(vector)
    first = jnp.dot(
        jnp.concatenate(parts, 0), high[...], preferred_element_type=jnp.float32
    )
    second = jnp.dot(
        jnp.concatenate(parts[:2], 0), middle[...], preferred_element_type=jnp.float32
    )
    third = jnp.dot(parts[0], low[...], preferred_element_type=jnp.float32)
    small = first[2 * COLS :] + second[COLS:] + third
    return first[:COLS] + (first[COLS : 2 * COLS] + second[:COLS] + small)


def mask_kernel(lists, masks):
    for side in range(2):
        for slot in range(HALO):
            for block in range(NB):
                chosen = jnp.full((SUBLANES, BS), lists[side, slot], jnp.int32) == block
                masks[side * HALO + slot, block] = jnp.where(chosen, 1.0, 0.0)


def operator_kernel(cols, blocks, *refs):
    own, received, dense = refs[:3], refs[3:6], refs[6]
    dense[...] = jnp.zeros_like(dense)
    for row in range(NB):
        for slot in range(blocks.shape[1]):
            start = pl.multiple_of(cols[row, slot] * BS, BS)
            place = (pl.ds(start, BS), slice(row * BS, (row + 1) * BS))
            dense[place] = dense[place] + blocks[row, slot].T
    unit = (
        lax.broadcasted_iota(jnp.int32, (BS, BS), 0) == lax.broadcasted_iota(jnp.int32, (BS, BS), 1)
    ).astype(jnp.float32)
    for row in range(NB):
        for column in range(EXT):
            place = (slice(column * BS, (column + 1) * BS), slice(row * BS, (row + 1) * BS))
            value = dense[place]
            if row == column:
                value = value - CENTER * unit
            targets = own if column < NB else received
            start = (column % NB) * BS
            for target, part in zip(targets, split(value * (1.0 / RADIUS))):
                target[start : start + BS, row * BS : (row + 1) * BS] = part


def write_chosen(masks, vector, to_next, to_previous):
    repeats = vector.shape[0] // SUBLANES
    for slot in range(HALO):
        for side, target in ((0, to_next), (1, to_previous)):
            total = None
            for block in range(NB):
                mask = jnp.concatenate([masks[side * HALO + slot, block]] * repeats, 0)
                value = vector[:, block * BS : (block + 1) * BS]
                total = value if total is None else jnp.where(mask > 0.5, value, total)
            target[:, slot * BS : (slot + 1) * BS] = total


def start_kernel(masks, parts, result, to_next, to_previous):
    vector = jnp.concatenate([parts[block] for block in range(NB)], 1)
    result[...] = vector
    write_chosen(masks, vector, to_next, to_previous)


def step_kernel(masks, partial, from_previous, from_next, *refs):
    parts, (result, to_next, to_previous) = refs[:3], refs[3:]
    received = jnp.concatenate([from_previous[...], from_next[...]], 1)
    vector = partial[...] + product(received, *parts)
    result[...] = vector
    write_chosen(masks, vector, to_next, to_previous)


def small_solve(matrix, target):
    count = len(target)
    lower = [[None] * count for unused in range(count)]
    inverse = [None] * count
    for outer in range(count):
        for inner in range(outer + 1):
            total = matrix[outer][inner]
            for other in range(inner):
                total = total - lower[outer][other] * lower[inner][other]
            if outer == inner:
                inverse[outer] = 1.0 / jnp.sqrt(total)
            else:
                lower[outer][inner] = total * inverse[inner]
    solved = []
    for outer in range(count):
        total = target[outer]
        for other in range(outer):
            total = total - lower[outer][other] * solved[other]
        solved.append(total * inverse[outer])
    result = [None] * count
    for outer in reversed(range(count)):
        total = solved[outer]
        for other in range(outer + 1, count):
            total = total - lower[other][outer] * result[other]
        result[outer] = total * inverse[outer]
    return result


def two_sum(left, right):
    total = left + right
    shadow = total - left
    return total, (left - (total - shadow)) + (right - shadow)


def coarse_split(value):
    grid = jnp.max(jnp.abs(value), 0, keepdims=True) * (1.5 * 2.0**15)
    coarse = (value + grid) - grid
    return coarse, value - coarse


def gram_row(vector, earlier):
    turned = jnp.concatenate([vector[:, i * BS : (i + 1) * BS] for i in range(NB)], 0).T
    coarse, rest = coarse_split(turned)
    row = []
    for other, other_rest in [*earlier, (coarse, rest)]:
        high = low = None
        for start in range(0, BS, SUBLANES):
            place = slice(start, start + SUBLANES)
            main = other[place] * coarse[place]
            side = other[place] * rest[place] + other_rest[place] * turned[place]
            high = main if high is None else high + main
            low = side if low is None else low + side
        row.append((high, low))
    return coarse, rest, row


def round_kernel(*refs):
    vector, parts, earlier = refs[0], refs[1:4], refs[4:-5]
    partial, coarse, rest, high, low = refs[-5:]
    value = vector[...]
    partial[...] = product(value, *parts)
    earlier = [(earlier[i], earlier[i + 1]) for i in range(0, len(earlier), 2)]
    coarse[...], rest[...], row = gram_row(value, earlier)
    for index, (one, other) in enumerate(row):
        high[index], low[index] = one, other


def pack_kernel(*refs):
    vector, earlier = refs[0], refs[1 : 1 + 2 * (COUNT - 1)]
    sums, packed = refs[1 + 2 * (COUNT - 1) : -1], refs[-1]
    earlier = [(earlier[i], earlier[i + 1]) for i in range(0, len(earlier), 2)]
    pairs = []
    for index in range(0, len(sums), 2):
        for i in range(sums[index].shape[0]):
            pairs.append((sums[index][i], sums[index + 1][i]))
    pairs += gram_row(vector[...], earlier)[2]
    sublane = lax.broadcasted_iota(jnp.int32, (SUBLANES, BS), 0)
    lane = lax.broadcasted_iota(jnp.int32, (SUBLANES, BS), 1) // COLS

    def folded(high, low, shift, axis):
        high, error = two_sum(high, pltpu.roll(high, shift, axis))
        return high, low + pltpu.roll(low, shift, axis) + error

    zero = jnp.zeros((SUBLANES, BS), jnp.float32)
    for tile in range(TILES):
        tile_high, tile_low = zero, zero
        for group in range(GROUP):
            high, low = zero, zero
            for row in range(SUBLANES):
                index = (tile * GROUP + group) * SUBLANES + row
                if index < len(pairs):
                    one, other = pairs[index]
                    for shift in (4, 2, 1):
                        one, other = folded(one, other, shift, 0)
                    high = jnp.where(sublane == row, one, high)
                    low = jnp.where(sublane == row, other, low)
            for shift in (2 * COLS, COLS):
                high, low = folded(high, low, shift, 1)
            tile_high = jnp.where(lane == group, high, tile_high)
            tile_low = jnp.where(lane == group, low, tile_low)
        tile_high, tile_low = two_sum(tile_high, tile_low)
        for copy in range(PART):
            packed[copy, tile * SUBLANES : (tile + 1) * SUBLANES] = tile_high
            packed[copy, SUM_ROWS + tile * SUBLANES : SUM_ROWS + (tile + 1) * SUBLANES] = tile_low


def summed(parts):
    high, low = parts[0, :SUM_ROWS], parts[0, SUM_ROWS:]
    for index in range(1, PART):
        high, error = two_sum(high, parts[index, :SUM_ROWS])
        low = low + parts[index, SUM_ROWS:] + error
    return two_sum(high, low)


def sum_kernel(parts, total):
    high, low = summed(parts)
    for copy in range(PART):
        total[copy, :SUM_ROWS] = high
        total[copy, SUM_ROWS:] = low


def halves(value):
    scaled = value * 4097.0
    high = scaled - (scaled - value)
    return high, value - high


def added_product(total, factor, value):
    factor, factor_high, factor_low = factor
    value, low, value_high, value_low = value
    main = factor_high * value_high
    side = factor_high * value_low + (factor_low * value + factor * low)
    if total is None:
        return main, side
    high, error = two_sum(total[0], main)
    return high, total[1] + (error + side)


def basis_gram(coefficients, gram):
    depth = gram[0][0].shape[0]
    index = lax.broadcasted_iota(jnp.int32, (depth, BS), 0)
    wide = [jnp.concatenate([value] * (depth // SUBLANES), 0) for value in coefficients]
    factors = [(value, *halves(value)) for value in wide]
    rows = []
    for i in range(STEPS + 1):
        total = None
        for a, factor in enumerate(factors):
            total = added_product(total, factor, gram[a + i])
        high, low = two_sum(*total)
        rows.append((high, low, *halves(high)))
    result = [[None] * (STEPS + 1) for unused in range(STEPS + 1)]
    for j in range(STEPS + 1):
        shifted = jnp.zeros((depth, BS), jnp.float32)
        for a, value in enumerate(wide):
            shifted = jnp.where(index == a + j, value, shifted)
        factor = (shifted, *halves(shifted))
        for i in range(j + 1):
            high, low = added_product(None, factor, rows[i])
            size = depth
            while size > SUBLANES:
                size //= 2
                high, error = two_sum(high[:size], high[size:])
                low = low[:size] + low[size:] + error
            for shift in (4, 2, 1):
                high, error = two_sum(high, pltpu.roll(high, shift, 0))
                low = low + pltpu.roll(low, shift, 0) + error
            result[i][j] = result[j][i] = high + low
    return result


def solved_weights(gram):
    combined = [
        [CENTER * gram[i][j] + RADIUS * gram[i + 1][j] for j in range(STEPS + 1)]
        for i in range(STEPS)
    ]
    normal = [
        [CENTER * combined[i][j] + RADIUS * combined[i][j + 1] for j in range(STEPS)]
        for i in range(STEPS)
    ]
    weights = small_solve(normal, [combined[i][0] for i in range(STEPS)])
    left = [1.0 - CENTER * weights[0]]
    for i in range(1, STEPS):
        left.append(-(CENTER * weights[i] + RADIUS * weights[i - 1]))
    left.append(-(RADIUS * weights[STEPS - 1]))
    return weights, left


def convolved(left, right):
    result = [None] * (len(left) + len(right) - 1)
    for i, one in enumerate(left):
        for j, other in enumerate(right):
            term = one * other
            result[i + j] = term if result[i + j] is None else result[i + j] + term
    return result


def all_cycles_kernel(fold, parts, *refs):
    vectors, own, other = refs[:COUNT], refs[COUNT], refs[COUNT + 1]
    high, low = summed(parts)
    rolled = [(high, low)]
    for group in range(1, GROUP):
        shift = BS - group * COLS
        rolled.append((pltpu.roll(high, shift, 1), pltpu.roll(low, shift, 1)))

    def entry(i, j):
        index = max(i, j) * (max(i, j) + 1) // 2 + min(i, j)
        tile, rest = divmod(index, SUBLANES * GROUP)
        group, row = divmod(rest, SUBLANES)
        row += tile * SUBLANES
        return [value[row : row + 1] for value in rolled[group]]

    depth = 2 * SUBLANES
    padding = [jnp.zeros((depth - COUNT, BS), jnp.float32)]
    gram = []
    for i in range(COUNT):
        entries = [entry(i, j) for j in range(COUNT)]
        value = jnp.concatenate([one for one, unused in entries] + padding, 0)
        rest = jnp.concatenate([one for unused, one in entries] + padding, 0)
        gram.append((value, rest, *halves(value)))

    def spread(value):
        return jnp.broadcast_to(value, (SUBLANES, BS))

    here = [[spread(entry(i, j)[0]) for j in range(STEPS + 1)] for i in range(STEPS + 1)]
    weights, polynomial = solved_weights(here)
    solution_part = list(weights)
    for cycle in range(1, CYCLES):
        here = basis_gram(polynomial, gram)
        weights, left = solved_weights(here)
        update = convolved(polynomial, weights)
        solution_part = [
            one + solution_part[i] if i < len(solution_part) else one
            for i, one in enumerate(update)
        ]
        polynomial = convolved(polynomial, left)
    remaining = None
    for i in range(STEPS + 1):
        for j in range(STEPS + 1):
            term = (left[i] * left[j]) * here[i][j]
            remaining = term if remaining is None else remaining + term
    reach = None
    for i in range(COUNT):
        term = jnp.abs(polynomial[i]) * jnp.sqrt(spread(entry(i, i)[0]))
        reach = term if reach is None else reach + term
    lane = lax.broadcasted_iota(jnp.int32, (SUBLANES, BS), 1)
    fine = (reach < LIMIT * jnp.sqrt(remaining)) | (lane >= COLS)
    bad = jnp.max(jnp.where(fine, 0.0, 1.0), axis=(0, 1), keepdims=True)
    other[2 * COLS :] = jnp.broadcast_to(bad, (SUBLANES, BS))
    index = lax.broadcasted_iota(jnp.int32, (depth, BS), 0)
    stacked = []
    for values in (solution_part, polynomial):
        total = jnp.zeros((depth, BS), jnp.float32)
        for i, value in enumerate(values):
            value = jnp.concatenate([value] * (depth // SUBLANES), 0)
            total = jnp.where(index == i, value, total)
        stacked.append(total)
    turned = jnp.concatenate(stacked, 0).T
    place = fold[0]
    partner = place + 1 - 2 * (place % 2)
    for output in range(2):
        sums = [None, None]
        for i in range(COUNT - 1 + output):
            column = output * depth + i
            weight = jnp.broadcast_to(turned[:COLS, column : column + 1], (COLS, BS))
            for side, block in enumerate((place, partner)):
                value = vectors[i][:, pl.ds(pl.multiple_of(block * BS, BS), BS)]
                term = weight * value
                sums[side] = term if sums[side] is None else sums[side] + term
        own[output * COLS : (output + 1) * COLS] = sums[0]
        other[output * COLS : (output + 1) * COLS] = sums[1]


def join_kernel(core, own, other, arrived, correction, residual, bad):
    for output, target in enumerate((correction, residual)):
        place = slice(output * COLS, (output + 1) * COLS)
        target[pl.ds(pl.multiple_of(core[0] * COLS, COLS), COLS)] = own[place]
        target[pl.ds(pl.multiple_of((1 - core[0]) * COLS, COLS), COLS)] = arrived[place]
    worst = jnp.max(jnp.maximum(other[2 * COLS :], arrived[2 * COLS :]))
    bad[0] = (worst > 0.5).astype(jnp.int32)


def call(kernel, out_shape, smem, vmem, scratch=(), flops=10**6, out_specs=None):
    return pl.pallas_call(
        kernel,
        out_shape=out_shape,
        in_specs=[SMEM] * len(smem) + [VMEM] * len(vmem),
        out_specs=out_specs or jax.tree.map(lambda unused: VMEM, out_shape),
        scratch_shapes=scratch,
        compiler_params=PARAMS,
        cost_estimate=pl.CostEstimate(flops=flops, bytes_accessed=2**20, transcendentals=0),
    )(*smem, *vmem)


def exchanged_over(groups):
    def exchanged(value):
        return lax.all_to_all(value, "sub", 0, 0, axis_index_groups=groups)

    return exchanged


def passed(value, by):
    subs = lax.axis_size("sub")
    return lax.ppermute(value, "sub", [(i, (i + by) % subs) for i in range(subs)])


VECTOR = f32(COLS, ROWS)
HALO_PART = f32(COLS, HALO * BS)


def cycle_by_cycle(right_side, blocks, block_cols, lists, fold):
    gathered = lax.all_gather(right_side, "fold", axis=0, tiled=True)

    def applied(vector):
        own = vector.reshape(NB, BS, -1)
        received = [passed(own[lists[0]], 1), passed(own[lists[1]], -1)]
        extended = jnp.concatenate([own, *received], 0)

        def added(slot, total):
            stored = lax.dynamic_index_in_dim(blocks, slot, 1, False)
            source = extended[lax.dynamic_index_in_dim(block_cols, slot, 1, False)]
            return total + jnp.einsum(
                "bij,bjc->bic", stored, source, precision=lax.Precision.HIGHEST
            )

        return lax.fori_loop(0, blocks.shape[1], added, jnp.zeros_like(own)).reshape(vector.shape)

    def grown(power, basis):
        latest = lax.dynamic_index_in_dim(basis, power, 0, False)
        following = (applied(latest) - CENTER * latest) / RADIUS
        return lax.dynamic_update_index_in_dim(basis, following, power + 1, 0)

    def cycle(unused, state):
        correction, residual = state
        basis = jnp.zeros((STEPS + 1,) + residual.shape, jnp.float32).at[0].set(residual)
        basis = lax.fori_loop(0, STEPS, grown, basis)
        gram = jnp.einsum("irc,jrc->ijc", basis, basis, precision=lax.Precision.HIGHEST)
        weights, left = solved_weights(lax.psum(gram, "sub"))
        correction = correction + sum(weights[i] * basis[i] for i in range(STEPS))
        return correction, sum(left[i] * basis[i] for i in range(STEPS + 1))

    results = lax.fori_loop(0, CYCLES, cycle, (jnp.zeros_like(gathered), gathered))
    return tuple(lax.dynamic_slice_in_dim(value, fold * BS, BS, 0).T for value in results)


def on_device(right_side, blocks, block_cols, send_lists):
    subs = lax.axis_size("sub")
    lists = send_lists[0]
    fold = lax.axis_index("fold").astype(jnp.int32)
    core = (fold % 2).reshape(1)
    halves_of_columns = right_side.T.reshape(2, COLS, BS)
    parts = lax.all_to_all(jnp.concatenate([halves_of_columns] * 2, 0), "fold", 0, 0)
    masks = call(mask_kernel, f32(2 * HALO, NB, SUBLANES, BS), [lists], [], flops=10**8)
    operator = call(
        operator_kernel,
        (bf16(ROWS, ROWS),) * 6,
        [block_cols],
        [blocks],
        [pltpu.VMEM((EXT * BS, ROWS), jnp.float32)],
        flops=10**9,
    )
    sends = call(start_kernel, (VECTOR, HALO_PART, HALO_PART), [], [masks, parts])
    square = f32(BS, BS)
    vectors, earlier, sums = [sends[0]], [], []
    for power in range(COUNT - 1):
        row = f32(power + 1, SUBLANES, BS)
        partial, coarse, rest, high, low = call(
            round_kernel,
            (VECTOR, square, square, row, row),
            [],
            [sends[0], *operator[:3], *earlier],
            flops=10**9,
        )
        earlier += [coarse, rest]
        sums += [high, low]
        received = [passed(sends[1], 1), passed(sends[2], -1)]
        sends = call(
            step_kernel,
            (VECTOR, HALO_PART, HALO_PART),
            [],
            [masks, partial, *received, *operator[3:]],
        )
        vectors.append(sends[0])
    packed = f32(PART, 2 * SUM_ROWS, BS)
    sums = call(pack_kernel, packed, [], [vectors[-1], *earlier, *sums])
    strided = [[i + PART * j for j in range(subs // PART)] for i in range(PART)]
    runs = [[PART * i + j for j in range(PART)] for i in range(subs // PART)]
    sums = call(sum_kernel, packed, [], [exchanged_over(strided)(sums)])
    own, other = call(
        all_cycles_kernel,
        (f32(2 * COLS, BS), f32(2 * COLS + SUBLANES, BS)),
        [fold.reshape(1)],
        [exchanged_over(runs)(sums), *vectors],
    )
    arrived = lax.ppermute(other, "fold", [(0, 1), (1, 0), (2, 3), (3, 2)])
    correction, residual, bad = call(
        join_kernel,
        (f32(2 * COLS, BS), f32(2 * COLS, BS), jax.ShapeDtypeStruct((1,), jnp.int32)),
        [core],
        [own, other, arrived],
        out_specs=(VMEM, VMEM, SMEM),
    )
    correction, residual = lax.cond(
        bad[0] > 0,
        lambda correction, residual, *rest: cycle_by_cycle(*rest),
        lambda correction, residual, *rest: (correction, residual),
        correction,
        residual,
        right_side,
        blocks,
        block_cols,
        lists,
        fold,
    )
    return (correction.T, residual.T)


def solution(mesh):
    placed = (
        P(("sub", "fold"), None),
        P("sub", None, None, None),
        P("sub", None),
        P("sub", None, None),
    )
    return jax.shard_map(
        on_device,
        mesh=mesh,
        in_specs=placed,
        out_specs=(P(("sub", "fold"), None), P(("sub", "fold"), None)),
        check_vma=False,
    )
```

```python
import functools

import jax
import jax.numpy as jnp
from jax import lax
from jax.experimental import pallas as pl
from jax.experimental.pallas import tpu as pltpu
from jax.sharding import PartitionSpec as P

STEPS = 4
CYCLES = 3
CENTER = 4.5
RADIUS = 3.5
BS = 128
NB = 4
HALO = 2
EXT = NB + 2 * HALO
ROWS = NB * BS
COLS = 32
PAIRS = [(i, j) for i in range(STEPS + 1) for j in range(i, STEPS + 1)]
GROUP = 128 // COLS
GRAM_ROWS = (len(PAIRS) + GROUP - 1) // GROUP

COUNT = STEPS * CYCLES + 1
SUBLANES = 8
PART = 8
TILES = -(-COUNT * (COUNT + 1) // 2 // (SUBLANES * GROUP))
SUM_ROWS = TILES * SUBLANES
LIMIT = 2000.0

VMEM = pl.BlockSpec(memory_space=pltpu.VMEM)
SMEM = pl.BlockSpec(memory_space=pltpu.SMEM)
PARAMS = pltpu.CompilerParams(vmem_limit_bytes=32 * 1024 * 1024)


def f32(*shape):
    return jax.ShapeDtypeStruct(shape, jnp.float32)


def bf16(*shape):
    return jax.ShapeDtypeStruct(shape, jnp.bfloat16)


def split(value):
    high = value.astype(jnp.bfloat16)
    value = value - high.astype(jnp.float32)
    middle = value.astype(jnp.bfloat16)
    low = (value - middle.astype(jnp.float32)).astype(jnp.bfloat16)
    return high, middle, low


def product(vector, high, middle, low):
    parts = split(vector)
    first = jnp.dot(
        jnp.concatenate(parts, 0), high[...], preferred_element_type=jnp.float32
    )
    second = jnp.dot(
        jnp.concatenate(parts[:2], 0), middle[...], preferred_element_type=jnp.float32
    )
    third = jnp.dot(parts[0], low[...], preferred_element_type=jnp.float32)
    small = first[2 * COLS :] + second[COLS:] + third
    return first[:COLS] + (first[COLS : 2 * COLS] + second[:COLS] + small)


def operator_kernel(cols, blocks, *refs):
    own, received, dense = refs[:3], refs[3:6], refs[6]
    turn = HALO * (lax.axis_index("sub") % 2)
    dense[...] = jnp.zeros_like(dense)
    for row in range(NB):
        for slot in range(blocks.shape[1]):
            column = cols[row, slot]
            swapped = NB + (column - NB + turn) % (2 * HALO)
            start = pl.multiple_of(jnp.where(column < NB, column, swapped) * BS, BS)
            place = (pl.ds(start, BS), slice(row * BS, (row + 1) * BS))
            dense[place] = dense[place] + blocks[row, slot].T
    unit = (
        lax.broadcasted_iota(jnp.int32, (BS, BS), 0) == lax.broadcasted_iota(jnp.int32, (BS, BS), 1)
    ).astype(jnp.float32)
    for row in range(NB):
        for column in range(EXT):
            place = (slice(column * BS, (column + 1) * BS), slice(row * BS, (row + 1) * BS))
            value = dense[place]
            if row == column:
                value = value - CENTER * unit
            targets = own if column < NB else received
            start = (column % NB) * BS
            for target, part in zip(targets, split(value * (1.0 / RADIUS))):
                target[start : start + BS, row * BS : (row + 1) * BS] = part


def write_chosen(masks, vector, sends):
    repeats = vector.shape[0] // SUBLANES
    for side, target in enumerate(sends):
        for slot in range(HALO):
            total = None
            for block in range(NB):
                mask = jnp.concatenate([masks[side * HALO + slot, block]] * repeats, 0)
                value = vector[:, block * BS : (block + 1) * BS]
                total = value if total is None else jnp.where(mask > 0.5, value, total)
            target[:, slot * BS : (slot + 1) * BS] = total


def start_kernel(lists, gathered, masks, result, *sends):
    parity = lax.axis_index("sub") % 2
    first = pl.multiple_of(lax.axis_index("fold") % 2 * COLS, COLS)
    for side in range(2):
        for slot in range(HALO):
            listed = lists[(side + parity + 1) % 2, slot]
            for block in range(NB):
                chosen = jnp.full((SUBLANES, BS), listed, jnp.int32) == block
                masks[side * HALO + slot, block] = jnp.where(chosen, 1.0, 0.0)
    vector = gathered[pl.ds(first, COLS), :]
    result[...] = vector
    write_chosen(masks, vector, sends)


def step_kernel(masks, partial, first, second, *refs):
    parts, (result, *sends) = refs[:3], refs[3:]
    received = jnp.concatenate([first[...], second[...]], 1)
    vector = partial[...] + product(received, *parts)
    result[...] = vector
    write_chosen(masks, vector, sends)


def small_solve(matrix, target):
    count = len(target)
    lower = [[None] * count for unused in range(count)]
    inverse = [None] * count
    for outer in range(count):
        for inner in range(outer + 1):
            total = matrix[outer][inner]
            for other in range(inner):
                total = total - lower[outer][other] * lower[inner][other]
            if outer == inner:
                inverse[outer] = 1.0 / jnp.sqrt(total)
            else:
                lower[outer][inner] = total * inverse[inner]
    solved = []
    for outer in range(count):
        total = target[outer]
        for other in range(outer):
            total = total - lower[outer][other] * solved[other]
        solved.append(total * inverse[outer])
    result = [None] * count
    for outer in reversed(range(count)):
        total = solved[outer]
        for other in range(outer + 1, count):
            total = total - lower[other][outer] * result[other]
        result[outer] = total * inverse[outer]
    return result


def two_sum(left, right):
    total = left + right
    shadow = total - left
    return total, (left - (total - shadow)) + (right - shadow)


def coarse_split(value):
    grid = jnp.max(jnp.abs(value), 0, keepdims=True) * (1.5 * 2.0**15)
    coarse = (value + grid) - grid
    return coarse, value - coarse


def gram_row(vector, earlier):
    turned = jnp.concatenate([vector[:, i * BS : (i + 1) * BS] for i in range(NB)], 0).T
    coarse, rest = coarse_split(turned)
    row = []
    for other, other_rest in [*earlier, (coarse, rest)]:
        high = low = None
        for start in range(0, BS, SUBLANES):
            place = slice(start, start + SUBLANES)
            main = other[place] * coarse[place]
            side = other[place] * rest[place] + other_rest[place] * turned[place]
            high = main if high is None else high + main
            low = side if low is None else low + side
        row.append((high, low))
    return coarse, rest, row


def round_kernel(*refs):
    vector, parts, earlier = refs[0], refs[1:4], refs[4:-5]
    partial, coarse, rest, high, low = refs[-5:]
    value = vector[...]
    partial[...] = product(value, *parts)
    earlier = [(earlier[i], earlier[i + 1]) for i in range(0, len(earlier), 2)]
    coarse[...], rest[...], row = gram_row(value, earlier)
    for index, (one, other) in enumerate(row):
        high[index], low[index] = one, other


def pack_kernel(*refs):
    vector, earlier = refs[0], refs[1 : 1 + 2 * (COUNT - 1)]
    sums, packed = refs[1 + 2 * (COUNT - 1) : -1], refs[-1]
    earlier = [(earlier[i], earlier[i + 1]) for i in range(0, len(earlier), 2)]
    pairs = []
    for index in range(0, len(sums), 2):
        for i in range(sums[index].shape[0]):
            pairs.append((sums[index][i], sums[index + 1][i]))
    pairs += gram_row(vector[...], earlier)[2]
    sublane = lax.broadcasted_iota(jnp.int32, (SUBLANES, BS), 0)
    lane = lax.broadcasted_iota(jnp.int32, (SUBLANES, BS), 1) // COLS

    def folded(high, low, shift, axis):
        high, error = two_sum(high, pltpu.roll(high, shift, axis))
        return high, low + pltpu.roll(low, shift, axis) + error

    zero = jnp.zeros((SUBLANES, BS), jnp.float32)
    for tile in range(TILES):
        tile_high, tile_low = zero, zero
        for group in range(GROUP):
            high, low = zero, zero
            for row in range(SUBLANES):
                index = (tile * GROUP + group) * SUBLANES + row
                if index < len(pairs):
                    one, other = pairs[index]
                    for shift in (4, 2, 1):
                        one, other = folded(one, other, shift, 0)
                    high = jnp.where(sublane == row, one, high)
                    low = jnp.where(sublane == row, other, low)
            for shift in (2 * COLS, COLS):
                high, low = folded(high, low, shift, 1)
            tile_high = jnp.where(lane == group, high, tile_high)
            tile_low = jnp.where(lane == group, low, tile_low)
        tile_high, tile_low = two_sum(tile_high, tile_low)
        for copy in range(PART):
            packed[copy, tile * SUBLANES : (tile + 1) * SUBLANES] = tile_high
            packed[copy, SUM_ROWS + tile * SUBLANES : SUM_ROWS + (tile + 1) * SUBLANES] = tile_low


def summed(parts):
    high, low = parts[0, :SUM_ROWS], parts[0, SUM_ROWS:]
    for index in range(1, PART):
        high, error = two_sum(high, parts[index, :SUM_ROWS])
        low = low + parts[index, SUM_ROWS:] + error
    return two_sum(high, low)


def sum_kernel(parts, total):
    high, low = summed(parts)
    for copy in range(PART):
        total[copy, :SUM_ROWS] = high
        total[copy, SUM_ROWS:] = low


def halves(value):
    scaled = value * 4097.0
    high = scaled - (scaled - value)
    return high, value - high


def added_product(total, factor, value):
    factor, factor_high, factor_low = factor
    value, low, value_high, value_low = value
    main = factor_high * value_high
    side = factor_high * value_low + (factor_low * value + factor * low)
    if total is None:
        return main, side
    high, error = two_sum(total[0], main)
    return high, total[1] + (error + side)


def basis_gram(coefficients, gram):
    depth = gram[0][0].shape[0]
    index = lax.broadcasted_iota(jnp.int32, (depth, BS), 0)
    wide = [jnp.concatenate([value] * (depth // SUBLANES), 0) for value in coefficients]
    factors = [(value, *halves(value)) for value in wide]
    rows = []
    for i in range(STEPS + 1):
        total = None
        for a, factor in enumerate(factors):
            total = added_product(total, factor, gram[a + i])
        high, low = two_sum(*total)
        rows.append((high, low, *halves(high)))
    result = [[None] * (STEPS + 1) for unused in range(STEPS + 1)]
    for j in range(STEPS + 1):
        shifted = jnp.zeros((depth, BS), jnp.float32)
        for a, value in enumerate(wide):
            shifted = jnp.where(index == a + j, value, shifted)
        factor = (shifted, *halves(shifted))
        for i in range(j + 1):
            high, low = added_product(None, factor, rows[i])
            size = depth
            while size > SUBLANES:
                size //= 2
                high, error = two_sum(high[:size], high[size:])
                low = low[:size] + low[size:] + error
            for shift in (4, 2, 1):
                high, error = two_sum(high, pltpu.roll(high, shift, 0))
                low = low + pltpu.roll(low, shift, 0) + error
            result[i][j] = result[j][i] = high + low
    return result


def solved_weights(gram):
    combined = [
        [CENTER * gram[i][j] + RADIUS * gram[i + 1][j] for j in range(STEPS + 1)]
        for i in range(STEPS)
    ]
    normal = [
        [CENTER * combined[i][j] + RADIUS * combined[i][j + 1] for j in range(STEPS)]
        for i in range(STEPS)
    ]
    weights = small_solve(normal, [combined[i][0] for i in range(STEPS)])
    left = [1.0 - CENTER * weights[0]]
    for i in range(1, STEPS):
        left.append(-(CENTER * weights[i] + RADIUS * weights[i - 1]))
    left.append(-(RADIUS * weights[STEPS - 1]))
    return weights, left


def convolved(left, right):
    result = [None] * (len(left) + len(right) - 1)
    for i, one in enumerate(left):
        for j, other in enumerate(right):
            term = one * other
            result[i + j] = term if result[i + j] is None else result[i + j] + term
    return result


def all_cycles_kernel(parts, *refs):
    vectors, own, other = refs[:COUNT], refs[COUNT], refs[COUNT + 1]
    high, low = summed(parts)
    rolled = [(high, low)]
    for group in range(1, GROUP):
        shift = BS - group * COLS
        rolled.append((pltpu.roll(high, shift, 1), pltpu.roll(low, shift, 1)))

    def entry(i, j):
        index = max(i, j) * (max(i, j) + 1) // 2 + min(i, j)
        tile, rest = divmod(index, SUBLANES * GROUP)
        group, row = divmod(rest, SUBLANES)
        row += tile * SUBLANES
        return [value[row : row + 1] for value in rolled[group]]

    depth = 2 * SUBLANES
    padding = [jnp.zeros((depth - COUNT, BS), jnp.float32)]
    gram = []
    for i in range(COUNT):
        entries = [entry(i, j) for j in range(COUNT)]
        value = jnp.concatenate([one for one, unused in entries] + padding, 0)
        rest = jnp.concatenate([one for unused, one in entries] + padding, 0)
        gram.append((value, rest, *halves(value)))

    def spread(value):
        return jnp.broadcast_to(value, (SUBLANES, BS))

    here = [[spread(entry(i, j)[0]) for j in range(STEPS + 1)] for i in range(STEPS + 1)]
    weights, polynomial = solved_weights(here)
    solution_part = list(weights)
    for cycle in range(1, CYCLES):
        here = basis_gram(polynomial, gram)
        weights, left = solved_weights(here)
        update = convolved(polynomial, weights)
        solution_part = [
            one + solution_part[i] if i < len(solution_part) else one
            for i, one in enumerate(update)
        ]
        polynomial = convolved(polynomial, left)
    remaining = None
    for i in range(STEPS + 1):
        for j in range(STEPS + 1):
            term = (left[i] * left[j]) * here[i][j]
            remaining = term if remaining is None else remaining + term
    reach = None
    for i in range(COUNT):
        term = jnp.abs(polynomial[i]) * jnp.sqrt(spread(entry(i, i)[0]))
        reach = term if reach is None else reach + term
    lane = lax.broadcasted_iota(jnp.int32, (SUBLANES, BS), 1)
    fine = (reach < LIMIT * jnp.sqrt(remaining)) | (lane >= COLS)
    bad = jnp.max(jnp.where(fine, 0.0, 1.0), axis=(0, 1), keepdims=True)
    other[2 * COLS :] = jnp.broadcast_to(bad, (SUBLANES, BS))
    index = lax.broadcasted_iota(jnp.int32, (depth, BS), 0)
    stacked = []
    for values in (solution_part, polynomial):
        total = jnp.zeros((depth, BS), jnp.float32)
        for i, value in enumerate(values):
            value = jnp.concatenate([value] * (depth // SUBLANES), 0)
            total = jnp.where(index == i, value, total)
        stacked.append(total)
    turned = jnp.concatenate(stacked, 0).T
    place = lax.axis_index("fold")
    partner = place + 1 - 2 * (place % 2)
    for output in range(2):
        sums = [None, None]
        for i in range(COUNT - 1 + output):
            column = output * depth + i
            weight = jnp.broadcast_to(turned[:COLS, column : column + 1], (COLS, BS))
            for side, block in enumerate((place, partner)):
                value = vectors[i][:, pl.ds(pl.multiple_of(block * BS, BS), BS)]
                term = weight * value
                sums[side] = term if sums[side] is None else sums[side] + term
        own[output * COLS : (output + 1) * COLS] = sums[0]
        other[output * COLS : (output + 1) * COLS] = sums[1]


def join_kernel(own, other, arrived, correction, residual, bad):
    core = lax.axis_index("fold") % 2
    for output, target in enumerate((correction, residual)):
        place = slice(output * COLS, (output + 1) * COLS)
        target[pl.ds(pl.multiple_of(core * COLS, COLS), COLS)] = own[place]
        target[pl.ds(pl.multiple_of((1 - core) * COLS, COLS), COLS)] = arrived[place]
    worst = jnp.max(jnp.maximum(other[2 * COLS :], arrived[2 * COLS :]))
    bad[0] = (worst > 0.5).astype(jnp.int32)


def call(kernel, out_shape, smem, vmem, scratch=(), flops=10**6, out_specs=None):
    return pl.pallas_call(
        kernel,
        out_shape=out_shape,
        in_specs=[SMEM] * len(smem) + [VMEM] * len(vmem),
        out_specs=out_specs or jax.tree.map(lambda unused: VMEM, out_shape),
        scratch_shapes=scratch,
        compiler_params=PARAMS,
        cost_estimate=pl.CostEstimate(flops=flops, bytes_accessed=2**20, transcendentals=0),
    )(*smem, *vmem)


def exchanged_over(groups):
    def exchanged(value):
        return lax.all_to_all(value, "sub", 0, 0, axis_index_groups=groups)

    return exchanged


def swapped(value, first):
    subs = lax.axis_size("sub")
    pairs = [(i, (i + 1) % subs) for i in range(first, subs, 2)]
    return lax.ppermute(value, "sub", pairs + [(j, i) for i, j in pairs])


def passed(value, by):
    subs = lax.axis_size("sub")
    return lax.ppermute(value, "sub", [(i, (i + by) % subs) for i in range(subs)])


VECTOR = f32(COLS, ROWS)
HALO_PART = f32(COLS, HALO * BS)


def cycle_by_cycle(right_side, blocks, block_cols, lists):
    gathered = lax.all_gather(right_side, "fold", axis=0, tiled=True)

    def applied(vector):
        own = vector.reshape(NB, BS, -1)
        received = [passed(own[lists[0]], 1), passed(own[lists[1]], -1)]
        extended = jnp.concatenate([own, *received], 0)

        def added(slot, total):
            stored = lax.dynamic_index_in_dim(blocks, slot, 1, False)
            source = extended[lax.dynamic_index_in_dim(block_cols, slot, 1, False)]
            return total + jnp.einsum(
                "bij,bjc->bic", stored, source, precision=lax.Precision.HIGHEST
            )

        return lax.fori_loop(0, blocks.shape[1], added, jnp.zeros_like(own)).reshape(vector.shape)

    def grown(power, basis):
        latest = lax.dynamic_index_in_dim(basis, power, 0, False)
        following = (applied(latest) - CENTER * latest) / RADIUS
        return lax.dynamic_update_index_in_dim(basis, following, power + 1, 0)

    def cycle(unused, state):
        correction, residual = state
        basis = jnp.zeros((STEPS + 1,) + residual.shape, jnp.float32).at[0].set(residual)
        basis = lax.fori_loop(0, STEPS, grown, basis)
        gram = jnp.einsum("irc,jrc->ijc", basis, basis, precision=lax.Precision.HIGHEST)
        weights, left = solved_weights(lax.psum(gram, "sub"))
        correction = correction + sum(weights[i] * basis[i] for i in range(STEPS))
        return correction, sum(left[i] * basis[i] for i in range(STEPS + 1))

    fold = lax.axis_index("fold")
    results = lax.fori_loop(0, CYCLES, cycle, (jnp.zeros_like(gathered), gathered))
    return tuple(lax.dynamic_slice_in_dim(value, fold * BS, BS, 0).T for value in results)


def on_device(right_side, blocks, block_cols, send_lists):
    subs = lax.axis_size("sub")
    lists = send_lists[0]
    gathered = lax.all_gather(right_side.T, "fold", axis=1, tiled=True)
    operator = call(
        operator_kernel,
        (bf16(ROWS, ROWS),) * 6,
        [block_cols],
        [blocks],
        [pltpu.VMEM((EXT * BS, ROWS), jnp.float32)],
        flops=10**9,
    )
    masks_shape = f32(2 * HALO, NB, SUBLANES, BS)
    masks, *sends = call(
        start_kernel, (masks_shape, VECTOR, HALO_PART, HALO_PART), [lists], [gathered]
    )
    square = f32(BS, BS)
    vectors, earlier, sums = [sends[0]], [], []
    for power in range(COUNT - 1):
        row = f32(power + 1, SUBLANES, BS)
        partial, coarse, rest, high, low = call(
            round_kernel,
            (VECTOR, square, square, row, row),
            [],
            [sends[0], *operator[:3], *earlier],
            flops=10**9,
        )
        earlier += [coarse, rest]
        sums += [high, low]
        received = [swapped(sends[1], 1), swapped(sends[2], 0)]
        sends = call(
            step_kernel,
            (VECTOR, HALO_PART, HALO_PART),
            [],
            [masks, partial, *received, *operator[3:]],
        )
        vectors.append(sends[0])
    packed = f32(PART, 2 * SUM_ROWS, BS)
    sums = call(pack_kernel, packed, [], [vectors[-1], *earlier, *sums])
    strided = [[i + PART * j for j in range(subs // PART)] for i in range(PART)]
    runs = [[PART * i + j for j in range(PART)] for i in range(subs // PART)]
    sums = call(sum_kernel, packed, [], [exchanged_over(strided)(sums)])
    own, other = call(
        all_cycles_kernel,
        (f32(2 * COLS, BS), f32(2 * COLS + SUBLANES, BS)),
        [],
        [exchanged_over(runs)(sums), *vectors],
    )
    arrived = lax.ppermute(other, "fold", [(0, 1), (1, 0), (2, 3), (3, 2)])
    correction, residual, bad = call(
        join_kernel,
        (f32(2 * COLS, BS), f32(2 * COLS, BS), jax.ShapeDtypeStruct((1,), jnp.int32)),
        [],
        [own, other, arrived],
        out_specs=(VMEM, VMEM, SMEM),
    )
    correction, residual = lax.cond(
        bad[0] > 0,
        lambda correction, residual, *rest: cycle_by_cycle(*rest),
        lambda correction, residual, *rest: (correction, residual),
        correction,
        residual,
        right_side,
        blocks,
        block_cols,
        lists,
    )
    return (correction.T, residual.T)


def solution(mesh):
    placed = (
        P(("sub", "fold"), None),
        P("sub", None, None, None),
        P("sub", None),
        P("sub", None, None),
    )
    return jax.shard_map(
        on_device,
        mesh=mesh,
        in_specs=placed,
        out_specs=(P(("sub", "fold"), None), P(("sub", "fold"), None)),
        check_vma=False,
    )
```

```python
import functools

import jax
import jax.numpy as jnp
from jax import lax
from jax.experimental import pallas as pl
from jax.experimental.pallas import tpu as pltpu
from jax.sharding import PartitionSpec as P

STEPS = 4
CYCLES = 3
CENTER = 4.5
RADIUS = 3.5
BS = 128
NB = 4
HALO = 2
EXT = NB + 2 * HALO
ROWS = NB * BS
COLS = 32
PAIRS = [(i, j) for i in range(STEPS + 1) for j in range(i, STEPS + 1)]
GROUP = 128 // COLS
GRAM_ROWS = (len(PAIRS) + GROUP - 1) // GROUP

COUNT = STEPS * CYCLES + 1
SUBLANES = 8
PART = 8
TILES = -(-COUNT * (COUNT + 1) // 2 // (SUBLANES * GROUP))
SUM_ROWS = TILES * SUBLANES
LIMIT = 2000.0
SINGLE = 4
CHUNKS = SINGLE - 1
SHARED = (EXT * BS + NB * SUBLANES) // CHUNKS

VMEM = pl.BlockSpec(memory_space=pltpu.VMEM)
SMEM = pl.BlockSpec(memory_space=pltpu.SMEM)
PARAMS = pltpu.CompilerParams(vmem_limit_bytes=32 * 1024 * 1024)


def f32(*shape):
    return jax.ShapeDtypeStruct(shape, jnp.float32)


def bf16(*shape):
    return jax.ShapeDtypeStruct(shape, jnp.bfloat16)


def split(value):
    high = value.astype(jnp.bfloat16)
    value = value - high.astype(jnp.float32)
    middle = value.astype(jnp.bfloat16)
    low = (value - middle.astype(jnp.float32)).astype(jnp.bfloat16)
    return high, middle, low


def product(vector, high, middle, low):
    parts = split(vector)
    first = jnp.dot(
        jnp.concatenate(parts, 0), high[...], preferred_element_type=jnp.float32
    )
    second = jnp.dot(
        jnp.concatenate(parts[:2], 0), middle[...], preferred_element_type=jnp.float32
    )
    third = jnp.dot(parts[0], low[...], preferred_element_type=jnp.float32)
    small = first[2 * COLS :] + second[COLS:] + third
    return first[:COLS] + (first[COLS : 2 * COLS] + second[:COLS] + small)


def sent_block(lists, side, slot):
    return lists[(side + lax.axis_index("sub") + 1) % 2, slot]


def chosen_block(listed, block):
    return jnp.where(jnp.full((SUBLANES, BS), listed, jnp.int32) == block, 1.0, 0.0)


def operator_kernel(cols, lists, blocks, *refs):
    own, received, chunks, dense = refs[:3], refs[3:6], refs[6:-1], refs[-1]
    turn = HALO * (lax.axis_index("sub") % 2)
    dense[...] = jnp.zeros_like(dense)
    for row in range(NB):
        for slot in range(blocks.shape[1]):
            column = cols[row, slot]
            swapped = NB + (column - NB + turn) % (2 * HALO)
            start = pl.multiple_of(jnp.where(column < NB, column, swapped) * BS, BS)
            place = (pl.ds(start, BS), slice(row * BS, (row + 1) * BS))
            dense[place] = dense[place] + blocks[row, slot].T
    unit = (
        lax.broadcasted_iota(jnp.int32, (BS, BS), 0) == lax.broadcasted_iota(jnp.int32, (BS, BS), 1)
    ).astype(jnp.float32)
    for row in range(NB):
        for column in range(EXT):
            place = (slice(column * BS, (column + 1) * BS), slice(row * BS, (row + 1) * BS))
            value = dense[place]
            if row == column:
                value = value - CENTER * unit
            value = value * (1.0 / RADIUS)
            dense[place] = value
            targets = own if column < NB else received
            start = (column % NB) * BS
            for target, part in zip(targets, split(value)):
                target[start : start + BS, row * BS : (row + 1) * BS] = part
    listed = sent_block(lists, 0, lax.axis_index("fold") % 2)
    masks = [chosen_block(listed, block) for block in range(NB)]
    start = pl.multiple_of(listed * BS, BS)
    shared = jnp.concatenate([dense[:, pl.ds(start, BS)], *masks], 0)
    for index, chunk in enumerate(chunks):
        chunk[...] = shared[index * SHARED : (index + 1) * SHARED]


def ghost_kernel(*refs):
    mine, others = (
        jnp.concatenate([ref[...] for ref in half], 0)
        for half in (refs[:CHUNKS], refs[CHUNKS : 2 * CHUNKS])
    )
    parts, masks = refs[2 * CHUNKS : -1], refs[-1]
    even = lax.axis_index("fold") % 2 == 0
    for slot in range(HALO):
        one, other = (mine, others) if slot == 0 else (others, mine)
        value = jnp.where(even, one, other)
        place = slice(slot * BS, (slot + 1) * BS)
        for target, part in zip(parts, split(value[: EXT * BS])):
            target[:, place] = part
        for block in range(NB):
            start = EXT * BS + block * SUBLANES
            masks[slot, block] = value[start : start + SUBLANES]


def write_chosen(masks, vector, target):
    repeats = vector.shape[0] // SUBLANES
    for slot in range(HALO):
        total = None
        for block in range(NB):
            mask = jnp.concatenate([masks[slot, block]] * repeats, 0)
            value = vector[:, block * BS : (block + 1) * BS]
            total = value if total is None else jnp.where(mask > 0.5, value, total)
        target[:, slot * BS : (slot + 1) * BS] = total


def write_sends(masks, vector, sends):
    for side, target in enumerate(sends):
        write_chosen(masks.at[side], vector, target)


def start_kernel(lists, gathered, masks, result, *sends):
    first = pl.multiple_of(lax.axis_index("fold") % 2 * COLS, COLS)
    for side in range(2):
        for slot in range(HALO):
            listed = sent_block(lists, side, slot)
            for block in range(NB):
                masks[side, slot, block] = chosen_block(listed, block)
    vector = gathered[pl.ds(first, COLS), :]
    result[...] = vector
    write_sends(masks, vector, sends)


def step_kernel(masks, partial, first, second, *refs):
    parts, (result, *sends) = refs[:3], refs[3:]
    received = jnp.concatenate([first[...], second[...]], 1)
    vector = partial[...] + product(received, *parts)
    result[...] = vector
    write_sends(masks, vector, sends)


def ahead_kernel(masks, partner_masks, partial, whole, across, near, sent, *refs):
    parts, ghost_parts, (result, send, ghost, first) = refs[:3], refs[3:6], refs[6:]
    write_chosen(partner_masks, whole, first)
    received = jnp.concatenate([first[...], near[...]], 1)
    vector = partial[...] + product(received, *parts)
    result[...] = vector
    write_chosen(masks.at[1], vector, send)
    extended = jnp.concatenate([whole[...], sent[...], across[...]], 1)
    ghost[...] = product(extended, *ghost_parts)


def small_solve(matrix, target):
    count = len(target)
    lower = [[None] * count for unused in range(count)]
    inverse = [None] * count
    for outer in range(count):
        for inner in range(outer + 1):
            total = matrix[outer][inner]
            for other in range(inner):
                total = total - lower[outer][other] * lower[inner][other]
            if outer == inner:
                inverse[outer] = 1.0 / jnp.sqrt(total)
            else:
                lower[outer][inner] = total * inverse[inner]
    solved = []
    for outer in range(count):
        total = target[outer]
        for other in range(outer):
            total = total - lower[outer][other] * solved[other]
        solved.append(total * inverse[outer])
    result = [None] * count
    for outer in reversed(range(count)):
        total = solved[outer]
        for other in range(outer + 1, count):
            total = total - lower[other][outer] * result[other]
        result[outer] = total * inverse[outer]
    return result


def two_sum(left, right):
    total = left + right
    shadow = total - left
    return total, (left - (total - shadow)) + (right - shadow)


def coarse_split(value):
    grid = jnp.max(jnp.abs(value), 0, keepdims=True) * (1.5 * 2.0**15)
    coarse = (value + grid) - grid
    return coarse, value - coarse


def gram_row(vector, earlier):
    turned = jnp.concatenate([vector[:, i * BS : (i + 1) * BS] for i in range(NB)], 0).T
    coarse, rest = coarse_split(turned)
    row = []
    for other, other_rest in [*earlier, (coarse, rest)]:
        high = low = None
        for start in range(0, BS, SUBLANES):
            place = slice(start, start + SUBLANES)
            main = other[place] * coarse[place]
            side = other[place] * rest[place] + other_rest[place] * turned[place]
            high = main if high is None else high + main
            low = side if low is None else low + side
        row.append((high, low))
    return coarse, rest, row


def round_kernel(*refs):
    vector, parts, earlier = refs[0], refs[1:4], refs[4:-5]
    partial, coarse, rest, high, low = refs[-5:]
    value = vector[...]
    partial[...] = product(value, *parts)
    earlier = [(earlier[i], earlier[i + 1]) for i in range(0, len(earlier), 2)]
    coarse[...], rest[...], row = gram_row(value, earlier)
    for index, (one, other) in enumerate(row):
        high[index], low[index] = one, other


def pack_kernel(*refs):
    vector, earlier = refs[0], refs[1 : 1 + 2 * (COUNT - 1)]
    sums, packed = refs[1 + 2 * (COUNT - 1) : -1], refs[-1]
    earlier = [(earlier[i], earlier[i + 1]) for i in range(0, len(earlier), 2)]
    pairs = []
    for index in range(0, len(sums), 2):
        for i in range(sums[index].shape[0]):
            pairs.append((sums[index][i], sums[index + 1][i]))
    pairs += gram_row(vector[...], earlier)[2]
    sublane = lax.broadcasted_iota(jnp.int32, (SUBLANES, BS), 0)
    lane = lax.broadcasted_iota(jnp.int32, (SUBLANES, BS), 1) // COLS

    def folded(high, low, shift, axis):
        high, error = two_sum(high, pltpu.roll(high, shift, axis))
        return high, low + pltpu.roll(low, shift, axis) + error

    zero = jnp.zeros((SUBLANES, BS), jnp.float32)
    for tile in range(TILES):
        tile_high, tile_low = zero, zero
        for group in range(GROUP):
            high, low = zero, zero
            for row in range(SUBLANES):
                index = (tile * GROUP + group) * SUBLANES + row
                if index < len(pairs):
                    one, other = pairs[index]
                    for shift in (4, 2, 1):
                        one, other = folded(one, other, shift, 0)
                    high = jnp.where(sublane == row, one, high)
                    low = jnp.where(sublane == row, other, low)
            for shift in (2 * COLS, COLS):
                high, low = folded(high, low, shift, 1)
            tile_high = jnp.where(lane == group, high, tile_high)
            tile_low = jnp.where(lane == group, low, tile_low)
        tile_high, tile_low = two_sum(tile_high, tile_low)
        for copy in range(PART):
            packed[copy, tile * SUBLANES : (tile + 1) * SUBLANES] = tile_high
            packed[copy, SUM_ROWS + tile * SUBLANES : SUM_ROWS + (tile + 1) * SUBLANES] = tile_low


def summed(parts):
    high, low = parts[0, :SUM_ROWS], parts[0, SUM_ROWS:]
    for index in range(1, PART):
        high, error = two_sum(high, parts[index, :SUM_ROWS])
        low = low + parts[index, SUM_ROWS:] + error
    return two_sum(high, low)


def sum_kernel(parts, total):
    high, low = summed(parts)
    for copy in range(PART):
        total[copy, :SUM_ROWS] = high
        total[copy, SUM_ROWS:] = low


def halves(value):
    scaled = value * 4097.0
    high = scaled - (scaled - value)
    return high, value - high


def added_product(total, factor, value):
    factor, factor_high, factor_low = factor
    value, low, value_high, value_low = value
    main = factor_high * value_high
    side = factor_high * value_low + (factor_low * value + factor * low)
    if total is None:
        return main, side
    high, error = two_sum(total[0], main)
    return high, total[1] + (error + side)


def basis_gram(coefficients, gram):
    depth = gram[0][0].shape[0]
    index = lax.broadcasted_iota(jnp.int32, (depth, BS), 0)
    wide = [jnp.concatenate([value] * (depth // SUBLANES), 0) for value in coefficients]
    factors = [(value, *halves(value)) for value in wide]
    rows = []
    for i in range(STEPS + 1):
        total = None
        for a, factor in enumerate(factors):
            total = added_product(total, factor, gram[a + i])
        high, low = two_sum(*total)
        rows.append((high, low, *halves(high)))
    result = [[None] * (STEPS + 1) for unused in range(STEPS + 1)]
    for j in range(STEPS + 1):
        shifted = jnp.zeros((depth, BS), jnp.float32)
        for a, value in enumerate(wide):
            shifted = jnp.where(index == a + j, value, shifted)
        factor = (shifted, *halves(shifted))
        for i in range(j + 1):
            high, low = added_product(None, factor, rows[i])
            size = depth
            while size > SUBLANES:
                size //= 2
                high, error = two_sum(high[:size], high[size:])
                low = low[:size] + low[size:] + error
            for shift in (4, 2, 1):
                high, error = two_sum(high, pltpu.roll(high, shift, 0))
                low = low + pltpu.roll(low, shift, 0) + error
            result[i][j] = result[j][i] = high + low
    return result


def solved_weights(gram):
    combined = [
        [CENTER * gram[i][j] + RADIUS * gram[i + 1][j] for j in range(STEPS + 1)]
        for i in range(STEPS)
    ]
    normal = [
        [CENTER * combined[i][j] + RADIUS * combined[i][j + 1] for j in range(STEPS)]
        for i in range(STEPS)
    ]
    weights = small_solve(normal, [combined[i][0] for i in range(STEPS)])
    left = [1.0 - CENTER * weights[0]]
    for i in range(1, STEPS):
        left.append(-(CENTER * weights[i] + RADIUS * weights[i - 1]))
    left.append(-(RADIUS * weights[STEPS - 1]))
    return weights, left


def convolved(left, right):
    result = [None] * (len(left) + len(right) - 1)
    for i, one in enumerate(left):
        for j, other in enumerate(right):
            term = one * other
            result[i + j] = term if result[i + j] is None else result[i + j] + term
    return result


def all_cycles_kernel(parts, *refs):
    vectors, own, other = refs[:COUNT], refs[COUNT], refs[COUNT + 1]
    high, low = summed(parts)
    rolled = [(high, low)]
    for group in range(1, GROUP):
        shift = BS - group * COLS
        rolled.append((pltpu.roll(high, shift, 1), pltpu.roll(low, shift, 1)))

    def entry(i, j):
        index = max(i, j) * (max(i, j) + 1) // 2 + min(i, j)
        tile, rest = divmod(index, SUBLANES * GROUP)
        group, row = divmod(rest, SUBLANES)
        row += tile * SUBLANES
        return [value[row : row + 1] for value in rolled[group]]

    depth = 2 * SUBLANES
    padding = [jnp.zeros((depth - COUNT, BS), jnp.float32)]
    gram = []
    for i in range(COUNT):
        entries = [entry(i, j) for j in range(COUNT)]
        value = jnp.concatenate([one for one, unused in entries] + padding, 0)
        rest = jnp.concatenate([one for unused, one in entries] + padding, 0)
        gram.append((value, rest, *halves(value)))

    def spread(value):
        return jnp.broadcast_to(value, (SUBLANES, BS))

    here = [[spread(entry(i, j)[0]) for j in range(STEPS + 1)] for i in range(STEPS + 1)]
    weights, polynomial = solved_weights(here)
    solution_part = list(weights)
    for cycle in range(1, CYCLES):
        here = basis_gram(polynomial, gram)
        weights, left = solved_weights(here)
        update = convolved(polynomial, weights)
        solution_part = [
            one + solution_part[i] if i < len(solution_part) else one
            for i, one in enumerate(update)
        ]
        polynomial = convolved(polynomial, left)
    remaining = None
    for i in range(STEPS + 1):
        for j in range(STEPS + 1):
            term = (left[i] * left[j]) * here[i][j]
            remaining = term if remaining is None else remaining + term
    reach = None
    for i in range(COUNT):
        term = jnp.abs(polynomial[i]) * jnp.sqrt(spread(entry(i, i)[0]))
        reach = term if reach is None else reach + term
    lane = lax.broadcasted_iota(jnp.int32, (SUBLANES, BS), 1)
    fine = (reach < LIMIT * jnp.sqrt(remaining)) | (lane >= COLS)
    bad = jnp.max(jnp.where(fine, 0.0, 1.0), axis=(0, 1), keepdims=True)
    other[2 * COLS :] = jnp.broadcast_to(bad, (SUBLANES, BS))
    index = lax.broadcasted_iota(jnp.int32, (depth, BS), 0)
    stacked = []
    for values in (solution_part, polynomial):
        total = jnp.zeros((depth, BS), jnp.float32)
        for i, value in enumerate(values):
            value = jnp.concatenate([value] * (depth // SUBLANES), 0)
            total = jnp.where(index == i, value, total)
        stacked.append(total)
    turned = jnp.concatenate(stacked, 0).T
    place = lax.axis_index("fold")
    partner = place + 1 - 2 * (place % 2)
    for output in range(2):
        sums = [None, None]
        for i in range(COUNT - 1 + output):
            column = output * depth + i
            weight = jnp.broadcast_to(turned[:COLS, column : column + 1], (COLS, BS))
            for side, block in enumerate((place, partner)):
                value = vectors[i][:, pl.ds(pl.multiple_of(block * BS, BS), BS)]
                term = weight * value
                sums[side] = term if sums[side] is None else sums[side] + term
        own[output * COLS : (output + 1) * COLS] = sums[0]
        other[output * COLS : (output + 1) * COLS] = sums[1]


def join_kernel(own, other, arrived, correction, residual, bad):
    core = lax.axis_index("fold") % 2
    for output, target in enumerate((correction, residual)):
        place = slice(output * COLS, (output + 1) * COLS)
        target[pl.ds(pl.multiple_of(core * COLS, COLS), COLS)] = own[place]
        target[pl.ds(pl.multiple_of((1 - core) * COLS, COLS), COLS)] = arrived[place]
    worst = jnp.max(jnp.maximum(other[2 * COLS :], arrived[2 * COLS :]))
    bad[0] = (worst > 0.5).astype(jnp.int32)


def call(kernel, out_shape, smem, vmem, scratch=(), flops=10**6, out_specs=None):
    return pl.pallas_call(
        kernel,
        out_shape=out_shape,
        in_specs=[SMEM] * len(smem) + [VMEM] * len(vmem),
        out_specs=out_specs or jax.tree.map(lambda unused: VMEM, out_shape),
        scratch_shapes=scratch,
        compiler_params=PARAMS,
        cost_estimate=pl.CostEstimate(flops=flops, bytes_accessed=2**20, transcendentals=0),
    )(*smem, *vmem)


def exchanged_over(groups):
    def exchanged(value):
        return lax.all_to_all(value, "sub", 0, 0, axis_index_groups=groups)

    return exchanged


def swapped(value, first):
    subs = lax.axis_size("sub")
    pairs = [(i, (i + 1) % subs) for i in range(first, subs, 2)]
    return lax.ppermute(value, "sub", pairs + [(j, i) for i, j in pairs])


def sent_across(value):
    subs = lax.axis_size("sub")
    pairs = [(i, (i + 2 if i % 2 == 0 else i - 2) % subs) for i in range(subs)]
    return lax.ppermute(value, "sub", pairs)


def core_swapped(value):
    return lax.ppermute(value, "fold", [(0, 1), (1, 0), (2, 3), (3, 2)])


def passed(value, by):
    subs = lax.axis_size("sub")
    return lax.ppermute(value, "sub", [(i, (i + by) % subs) for i in range(subs)])


VECTOR = f32(COLS, ROWS)
HALO_PART = f32(COLS, HALO * BS)


def cycle_by_cycle(right_side, blocks, block_cols, lists):
    gathered = lax.all_gather(right_side, "fold", axis=0, tiled=True)

    def applied(vector):
        own = vector.reshape(NB, BS, -1)
        received = [passed(own[lists[0]], 1), passed(own[lists[1]], -1)]
        extended = jnp.concatenate([own, *received], 0)

        def added(slot, total):
            stored = lax.dynamic_index_in_dim(blocks, slot, 1, False)
            source = extended[lax.dynamic_index_in_dim(block_cols, slot, 1, False)]
            return total + jnp.einsum(
                "bij,bjc->bic", stored, source, precision=lax.Precision.HIGHEST
            )

        return lax.fori_loop(0, blocks.shape[1], added, jnp.zeros_like(own)).reshape(vector.shape)

    def grown(power, basis):
        latest = lax.dynamic_index_in_dim(basis, power, 0, False)
        following = (applied(latest) - CENTER * latest) / RADIUS
        return lax.dynamic_update_index_in_dim(basis, following, power + 1, 0)

    def cycle(unused, state):
        correction, residual = state
        basis = jnp.zeros((STEPS + 1,) + residual.shape, jnp.float32).at[0].set(residual)
        basis = lax.fori_loop(0, STEPS, grown, basis)
        gram = jnp.einsum("irc,jrc->ijc", basis, basis, precision=lax.Precision.HIGHEST)
        weights, left = solved_weights(lax.psum(gram, "sub"))
        correction = correction + sum(weights[i] * basis[i] for i in range(STEPS))
        return correction, sum(left[i] * basis[i] for i in range(STEPS + 1))

    fold = lax.axis_index("fold")
    results = lax.fori_loop(0, CYCLES, cycle, (jnp.zeros_like(gathered), gathered))
    return tuple(lax.dynamic_slice_in_dim(value, fold * BS, BS, 0).T for value in results)


def on_device(right_side, blocks, block_cols, send_lists):
    subs = lax.axis_size("sub")
    lists = send_lists[0]
    gathered = lax.all_gather(right_side.T, "fold", axis=1, tiled=True)
    operator = call(
        operator_kernel,
        (bf16(ROWS, ROWS),) * 6 + (f32(SHARED, BS),) * CHUNKS,
        [block_cols, lists],
        [blocks],
        [pltpu.VMEM((EXT * BS, ROWS), jnp.float32)],
        flops=10**9,
    )
    operator, chunks = operator[:6], operator[6:]
    masks_shape = f32(2, HALO, NB, SUBLANES, BS)
    masks, *sends = call(
        start_kernel, (masks_shape, VECTOR, HALO_PART, HALO_PART), [lists], [gathered]
    )
    square = f32(BS, BS)
    vectors, earlier, sums = [], [], []

    def own_part(vector):
        row = f32(len(vectors) + 1, SUBLANES, BS)
        partial, coarse, rest, high, low = call(
            round_kernel,
            (VECTOR, square, square, row, row),
            [],
            [vector, *operator[:3], *earlier],
            flops=10**9,
        )
        vectors.append(vector)
        earlier.extend([coarse, rest])
        sums.extend([high, low])
        return partial

    def stepped(partial, first, second):
        return list(
            call(
                step_kernel,
                (VECTOR, HALO_PART, HALO_PART),
                [],
                [masks, partial, first, second, *operator[3:]],
            )
        )

    shared = []
    for power in range(SINGLE):
        if power < CHUNKS:
            chunk, partial = lax.optimization_barrier((chunks[power], own_part(sends[0])))
            shared.append(swapped(chunk, 1))
        else:
            shared, sends[0] = lax.optimization_barrier((shared, sends[0]))
            others = [core_swapped(chunk) for chunk in shared]
            partial = own_part(sends[0])
        sends = stepped(partial, swapped(sends[1], 1), swapped(sends[2], 0))
    *ghost_operator, partner_masks = call(
        ghost_kernel,
        (bf16(EXT * BS, HALO * BS),) * 3 + (f32(HALO, NB, SUBLANES, BS),),
        [],
        [*shared, *others],
        flops=10**8,
    )
    for power in range(SINGLE, COUNT - 1, 2):
        vector, between, within = sends
        partial = own_part(vector)
        arrived = [swapped(vector, 1), sent_across(within), swapped(within, 0)]
        vector, within, ghost = call(
            ahead_kernel,
            (VECTOR, HALO_PART, HALO_PART),
            [],
            [masks, partner_masks, partial, *arrived, between, *operator[3:], *ghost_operator],
            [pltpu.VMEM((COLS, HALO * BS), jnp.float32)],
        )
        partial = own_part(vector)
        sends = stepped(partial, ghost, swapped(within, 0))
    vectors.append(sends[0])
    packed = f32(PART, 2 * SUM_ROWS, BS)
    sums = call(pack_kernel, packed, [], [vectors[-1], *earlier, *sums])
    strided = [[i + PART * j for j in range(subs // PART)] for i in range(PART)]
    runs = [[PART * i + j for j in range(PART)] for i in range(subs // PART)]
    sums = call(sum_kernel, packed, [], [exchanged_over(strided)(sums)])
    own, other = call(
        all_cycles_kernel,
        (f32(2 * COLS, BS), f32(2 * COLS + SUBLANES, BS)),
        [],
        [exchanged_over(runs)(sums), *vectors],
    )
    arrived = core_swapped(other)
    correction, residual, bad = call(
        join_kernel,
        (f32(2 * COLS, BS), f32(2 * COLS, BS), jax.ShapeDtypeStruct((1,), jnp.int32)),
        [],
        [own, other, arrived],
        out_specs=(VMEM, VMEM, SMEM),
    )
    correction, residual = lax.cond(
        bad[0] > 0,
        lambda correction, residual, *rest: cycle_by_cycle(*rest),
        lambda correction, residual, *rest: (correction, residual),
        correction,
        residual,
        right_side,
        blocks,
        block_cols,
        lists,
    )
    return (correction.T, residual.T)


def solution(mesh):
    placed = (
        P(("sub", "fold"), None),
        P("sub", None, None, None),
        P("sub", None),
        P("sub", None, None),
    )
    return jax.shard_map(
        on_device,
        mesh=mesh,
        in_specs=placed,
        out_specs=(P(("sub", "fold"), None), P(("sub", "fold"), None)),
        check_vma=False,
    )
```

```python
import functools

import jax
import jax.numpy as jnp
from jax import lax
from jax.experimental import pallas as pl
from jax.experimental.pallas import tpu as pltpu
from jax.sharding import PartitionSpec as P

STEPS = 4
CYCLES = 3
CENTER = 4.5
RADIUS = 3.5
BS = 128
NB = 4
HALO = 2
EXT = NB + 2 * HALO
ROWS = NB * BS
COLS = 32
PAIRS = [(i, j) for i in range(STEPS + 1) for j in range(i, STEPS + 1)]
GROUP = 128 // COLS
GRAM_ROWS = (len(PAIRS) + GROUP - 1) // GROUP

COUNT = STEPS * CYCLES + 1
SUBLANES = 8
PART = 8
TILES = -(-COUNT * (COUNT + 1) // 2 // (SUBLANES * GROUP))
SUM_ROWS = TILES * SUBLANES
LIMIT = 2000.0
SINGLE = 4
CHUNKS = SINGLE - 1
SHARED = (EXT * BS + NB * SUBLANES) // CHUNKS

VMEM = pl.BlockSpec(memory_space=pltpu.VMEM)
SMEM = pl.BlockSpec(memory_space=pltpu.SMEM)
PARAMS = pltpu.CompilerParams(vmem_limit_bytes=32 * 1024 * 1024)


def f32(*shape):
    return jax.ShapeDtypeStruct(shape, jnp.float32)


def bf16(*shape):
    return jax.ShapeDtypeStruct(shape, jnp.bfloat16)


def split(value):
    high = value.astype(jnp.bfloat16)
    value = value - high.astype(jnp.float32)
    middle = value.astype(jnp.bfloat16)
    low = (value - middle.astype(jnp.float32)).astype(jnp.bfloat16)
    return high, middle, low


def product(vector, high, middle, low):
    parts = split(vector)
    first = jnp.dot(
        jnp.concatenate(parts, 0), high[...], preferred_element_type=jnp.float32
    )
    second = jnp.dot(
        jnp.concatenate(parts[:2], 0), middle[...], preferred_element_type=jnp.float32
    )
    third = jnp.dot(parts[0], low[...], preferred_element_type=jnp.float32)
    small = first[2 * COLS :] + second[COLS:] + third
    return first[:COLS] + (first[COLS : 2 * COLS] + second[:COLS] + small)


def sent_block(lists, side, slot):
    return lists[(side + lax.axis_index("sub") + 1) % 2, slot]


def chosen_block(listed, block):
    return jnp.where(jnp.full((SUBLANES, BS), listed, jnp.int32) == block, 1.0, 0.0)


def operator_kernel(cols, lists, blocks, *refs):
    own, received, chunks, dense = refs[:3], refs[3:6], refs[6:-1], refs[-1]
    turn = HALO * (lax.axis_index("sub") % 2)
    dense[...] = jnp.zeros_like(dense)
    for row in range(NB):
        for slot in range(blocks.shape[1]):
            column = cols[row, slot]
            swapped = NB + (column - NB + turn) % (2 * HALO)
            start = pl.multiple_of(jnp.where(column < NB, column, swapped) * BS, BS)
            place = (pl.ds(start, BS), slice(row * BS, (row + 1) * BS))
            dense[place] = dense[place] + blocks[row, slot].T
    unit = (
        lax.broadcasted_iota(jnp.int32, (BS, BS), 0) == lax.broadcasted_iota(jnp.int32, (BS, BS), 1)
    ).astype(jnp.float32)
    for row in range(NB):
        for column in range(EXT):
            place = (slice(column * BS, (column + 1) * BS), slice(row * BS, (row + 1) * BS))
            value = dense[place]
            if row == column:
                value = value - CENTER * unit
            value = value * (1.0 / RADIUS)
            dense[place] = value
            targets = own if column < NB else received
            start = (column % NB) * BS
            for target, part in zip(targets, split(value)):
                target[start : start + BS, row * BS : (row + 1) * BS] = part
    listed = sent_block(lists, 0, lax.axis_index("fold") % 2)
    masks = [chosen_block(listed, block) for block in range(NB)]
    start = pl.multiple_of(listed * BS, BS)
    shared = jnp.concatenate([dense[:, pl.ds(start, BS)], *masks], 0)
    for index, chunk in enumerate(chunks):
        chunk[...] = shared[index * SHARED : (index + 1) * SHARED]


def ghost_kernel(*refs):
    mine, others = (
        jnp.concatenate([ref[...] for ref in half], 0)
        for half in (refs[:CHUNKS], refs[CHUNKS : 2 * CHUNKS])
    )
    parts, masks = refs[2 * CHUNKS : -1], refs[-1]
    even = lax.axis_index("fold") % 2 == 0
    for slot in range(HALO):
        one, other = (mine, others) if slot == 0 else (others, mine)
        value = jnp.where(even, one, other)
        place = slice(slot * BS, (slot + 1) * BS)
        for target, part in zip(parts, split(value[: EXT * BS])):
            target[:, place] = part
        for block in range(NB):
            start = EXT * BS + block * SUBLANES
            masks[slot, block] = value[start : start + SUBLANES]


def write_chosen(masks, vector, target):
    repeats = vector.shape[0] // SUBLANES
    for slot in range(HALO):
        total = None
        for block in range(NB):
            mask = jnp.concatenate([masks[slot, block]] * repeats, 0)
            value = vector[:, block * BS : (block + 1) * BS]
            total = value if total is None else jnp.where(mask > 0.5, value, total)
        target[:, slot * BS : (slot + 1) * BS] = total


def write_sends(masks, vector, sends):
    for side, target in enumerate(sends):
        write_chosen(masks.at[side], vector, target)


def start_kernel(lists, gathered, masks, result, *sends):
    first = pl.multiple_of(lax.axis_index("fold") % 2 * COLS, COLS)
    for side in range(2):
        for slot in range(HALO):
            listed = sent_block(lists, side, slot)
            for block in range(NB):
                masks[side, slot, block] = chosen_block(listed, block)
    vector = gathered[pl.ds(first, COLS), :]
    result[...] = vector
    write_sends(masks, vector, sends)


def step_kernel(masks, partial, first, second, *refs):
    parts, (result, *sends) = refs[:3], refs[3:]
    received = jnp.concatenate([first[...], second[...]], 1)
    vector = partial[...] + product(received, *parts)
    result[...] = vector
    write_sends(masks, vector, sends)


def ahead_kernel(masks, partner_masks, partial, whole, across, near, sent, *refs):
    parts, ghost_parts, (result, send, ghost, first) = refs[:3], refs[3:6], refs[6:]
    write_chosen(partner_masks, whole, first)
    received = jnp.concatenate([first[...], near[...]], 1)
    vector = partial[...] + product(received, *parts)
    result[...] = vector
    write_chosen(masks.at[1], vector, send)
    extended = jnp.concatenate([whole[...], sent[...], across[...]], 1)
    ghost[...] = product(extended, *ghost_parts)


def small_solve(matrix, target):
    count = len(target)
    lower = [[None] * count for unused in range(count)]
    inverse = [None] * count
    for outer in range(count):
        for inner in range(outer + 1):
            total = matrix[outer][inner]
            for other in range(inner):
                total = total - lower[outer][other] * lower[inner][other]
            if outer == inner:
                inverse[outer] = 1.0 / jnp.sqrt(total)
            else:
                lower[outer][inner] = total * inverse[inner]
    solved = []
    for outer in range(count):
        total = target[outer]
        for other in range(outer):
            total = total - lower[outer][other] * solved[other]
        solved.append(total * inverse[outer])
    result = [None] * count
    for outer in reversed(range(count)):
        total = solved[outer]
        for other in range(outer + 1, count):
            total = total - lower[other][outer] * result[other]
        result[outer] = total * inverse[outer]
    return result


def two_sum(left, right):
    total = left + right
    shadow = total - left
    return total, (left - (total - shadow)) + (right - shadow)


def coarse_split(value):
    grid = jnp.max(jnp.abs(value), 0, keepdims=True) * (1.5 * 2.0**15)
    coarse = (value + grid) - grid
    return coarse, value - coarse


def gram_row(vector, earlier):
    turned = jnp.concatenate([vector[:, i * BS : (i + 1) * BS] for i in range(NB)], 0).T
    coarse, rest = coarse_split(turned)
    row = []
    for other, other_rest in [*earlier, (coarse, rest)]:
        high = low = None
        for start in range(0, BS, SUBLANES):
            place = slice(start, start + SUBLANES)
            main = other[place] * coarse[place]
            side = other[place] * rest[place] + other_rest[place] * turned[place]
            high = main if high is None else high + main
            low = side if low is None else low + side
        row.append((high, low))
    return coarse, rest, row


def round_kernel(*refs):
    vector, parts, earlier = refs[0], refs[1:4], refs[4:-5]
    partial, coarse, rest, high, low = refs[-5:]
    value = vector[...]
    partial[...] = product(value, *parts)
    earlier = [(earlier[i], earlier[i + 1]) for i in range(0, len(earlier), 2)]
    coarse[...], rest[...], row = gram_row(value, earlier)
    for index, (one, other) in enumerate(row):
        high[index], low[index] = one, other


def pack_kernel(*refs):
    vector, earlier = refs[0], refs[1 : 1 + 2 * (COUNT - 1)]
    sums, packed = refs[1 + 2 * (COUNT - 1) : -1], refs[-1]
    earlier = [(earlier[i], earlier[i + 1]) for i in range(0, len(earlier), 2)]
    pairs = []
    for index in range(0, len(sums), 2):
        for i in range(sums[index].shape[0]):
            pairs.append((sums[index][i], sums[index + 1][i]))
    pairs += gram_row(vector[...], earlier)[2]
    sublane = lax.broadcasted_iota(jnp.int32, (SUBLANES, BS), 0)
    lane = lax.broadcasted_iota(jnp.int32, (SUBLANES, BS), 1) // COLS

    def folded(high, low, shift, axis):
        high, error = two_sum(high, pltpu.roll(high, shift, axis))
        return high, low + pltpu.roll(low, shift, axis) + error

    zero = jnp.zeros((SUBLANES, BS), jnp.float32)
    for tile in range(TILES):
        tile_high, tile_low = zero, zero
        for group in range(GROUP):
            high, low = zero, zero
            for row in range(SUBLANES):
                index = (tile * GROUP + group) * SUBLANES + row
                if index < len(pairs):
                    one, other = pairs[index]
                    for shift in (4, 2, 1):
                        one, other = folded(one, other, shift, 0)
                    high = jnp.where(sublane == row, one, high)
                    low = jnp.where(sublane == row, other, low)
            for shift in (2 * COLS, COLS):
                high, low = folded(high, low, shift, 1)
            tile_high = jnp.where(lane == group, high, tile_high)
            tile_low = jnp.where(lane == group, low, tile_low)
        tile_high, tile_low = two_sum(tile_high, tile_low)
        for copy in range(PART):
            packed[copy, tile * SUBLANES : (tile + 1) * SUBLANES] = tile_high
            packed[copy, SUM_ROWS + tile * SUBLANES : SUM_ROWS + (tile + 1) * SUBLANES] = tile_low


def summed(parts):
    high, low = parts[0, :SUM_ROWS], parts[0, SUM_ROWS:]
    for index in range(1, PART):
        high, error = two_sum(high, parts[index, :SUM_ROWS])
        low = low + parts[index, SUM_ROWS:] + error
    return two_sum(high, low)


def sum_kernel(parts, total):
    high, low = summed(parts)
    for copy in range(PART):
        total[copy, :SUM_ROWS] = high
        total[copy, SUM_ROWS:] = low


def halves(value):
    scaled = value * 4097.0
    high = scaled - (scaled - value)
    return high, value - high


def added_product(total, factor, value):
    factor, factor_high, factor_low = factor
    value, low, value_high, value_low = value
    main = factor_high * value_high
    side = factor_high * value_low + (factor_low * value + factor * low)
    if total is None:
        return main, side
    high, error = two_sum(total[0], main)
    return high, total[1] + (error + side)


def basis_gram(coefficients, gram):
    depth = gram[0][0].shape[0]
    index = lax.broadcasted_iota(jnp.int32, (depth, BS), 0)
    wide = [jnp.concatenate([value] * (depth // SUBLANES), 0) for value in coefficients]
    factors = [(value, *halves(value)) for value in wide]
    rows = []
    for i in range(STEPS + 1):
        total = None
        for a, factor in enumerate(factors):
            total = added_product(total, factor, gram[a + i])
        high, low = two_sum(*total)
        rows.append((high, low, *halves(high)))
    result = [[None] * (STEPS + 1) for unused in range(STEPS + 1)]
    for j in range(STEPS + 1):
        shifted = jnp.zeros((depth, BS), jnp.float32)
        for a, value in enumerate(wide):
            shifted = jnp.where(index == a + j, value, shifted)
        factor = (shifted, *halves(shifted))
        for i in range(j + 1):
            high, low = added_product(None, factor, rows[i])
            size = depth
            while size > SUBLANES:
                size //= 2
                high, error = two_sum(high[:size], high[size:])
                low = low[:size] + low[size:] + error
            for shift in (4, 2, 1):
                high, error = two_sum(high, pltpu.roll(high, shift, 0))
                low = low + pltpu.roll(low, shift, 0) + error
            result[i][j] = result[j][i] = high + low
    return result


def solved_weights(gram):
    combined = [
        [CENTER * gram[i][j] + RADIUS * gram[i + 1][j] for j in range(STEPS + 1)]
        for i in range(STEPS)
    ]
    normal = [
        [CENTER * combined[i][j] + RADIUS * combined[i][j + 1] for j in range(STEPS)]
        for i in range(STEPS)
    ]
    weights = small_solve(normal, [combined[i][0] for i in range(STEPS)])
    left = [1.0 - CENTER * weights[0]]
    for i in range(1, STEPS):
        left.append(-(CENTER * weights[i] + RADIUS * weights[i - 1]))
    left.append(-(RADIUS * weights[STEPS - 1]))
    return weights, left


def convolved(left, right):
    result = [None] * (len(left) + len(right) - 1)
    for i, one in enumerate(left):
        for j, other in enumerate(right):
            term = one * other
            result[i + j] = term if result[i + j] is None else result[i + j] + term
    return result


def all_cycles_kernel(parts, *refs):
    vectors, own, other = refs[:COUNT], refs[COUNT], refs[COUNT + 1]
    high, low = summed(parts)
    rolled = [(high, low)]
    for group in range(1, GROUP):
        shift = BS - group * COLS
        rolled.append((pltpu.roll(high, shift, 1), pltpu.roll(low, shift, 1)))

    def entry(i, j):
        index = max(i, j) * (max(i, j) + 1) // 2 + min(i, j)
        tile, rest = divmod(index, SUBLANES * GROUP)
        group, row = divmod(rest, SUBLANES)
        row += tile * SUBLANES
        return [value[row : row + 1] for value in rolled[group]]

    depth = 2 * SUBLANES
    padding = [jnp.zeros((depth - COUNT, BS), jnp.float32)]
    gram = []
    for i in range(COUNT):
        entries = [entry(i, j) for j in range(COUNT)]
        value = jnp.concatenate([one for one, unused in entries] + padding, 0)
        rest = jnp.concatenate([one for unused, one in entries] + padding, 0)
        gram.append((value, rest, *halves(value)))

    def spread(value):
        return jnp.broadcast_to(value, (SUBLANES, BS))

    here = [[spread(entry(i, j)[0]) for j in range(STEPS + 1)] for i in range(STEPS + 1)]
    weights, polynomial = solved_weights(here)
    solution_part = list(weights)
    for cycle in range(1, CYCLES):
        here = basis_gram(polynomial, gram)
        weights, left = solved_weights(here)
        update = convolved(polynomial, weights)
        solution_part = [
            one + solution_part[i] if i < len(solution_part) else one
            for i, one in enumerate(update)
        ]
        polynomial = convolved(polynomial, left)
    remaining = None
    for i in range(STEPS + 1):
        for j in range(STEPS + 1):
            term = (left[i] * left[j]) * here[i][j]
            remaining = term if remaining is None else remaining + term
    reach = None
    for i in range(COUNT):
        term = jnp.abs(polynomial[i]) * jnp.sqrt(spread(entry(i, i)[0]))
        reach = term if reach is None else reach + term
    lane = lax.broadcasted_iota(jnp.int32, (SUBLANES, BS), 1)
    fine = (reach < LIMIT * jnp.sqrt(remaining)) | (lane >= COLS)
    bad = jnp.max(jnp.where(fine, 0.0, 1.0), axis=(0, 1), keepdims=True)
    other[2 * COLS :] = jnp.broadcast_to(bad, (SUBLANES, BS))
    index = lax.broadcasted_iota(jnp.int32, (depth, BS), 0)
    stacked = []
    for values in (solution_part, polynomial):
        total = jnp.zeros((depth, BS), jnp.float32)
        for i, value in enumerate(values):
            value = jnp.concatenate([value] * (depth // SUBLANES), 0)
            total = jnp.where(index == i, value, total)
        stacked.append(total)
    turned = jnp.concatenate(stacked, 0).T
    place = lax.axis_index("fold")
    partner = place + 1 - 2 * (place % 2)
    for output in range(2):
        sums = [None, None]
        for i in range(COUNT - 1 + output):
            column = output * depth + i
            weight = jnp.broadcast_to(turned[:COLS, column : column + 1], (COLS, BS))
            for side, block in enumerate((place, partner)):
                value = vectors[i][:, pl.ds(pl.multiple_of(block * BS, BS), BS)]
                term = weight * value
                sums[side] = term if sums[side] is None else sums[side] + term
        own[output * COLS : (output + 1) * COLS] = sums[0]
        other[output * COLS : (output + 1) * COLS] = sums[1]


def join_kernel(own, other, arrived, correction, residual, bad):
    core = lax.axis_index("fold") % 2
    for output, target in enumerate((correction, residual)):
        place = slice(output * COLS, (output + 1) * COLS)
        target[pl.ds(pl.multiple_of(core * COLS, COLS), COLS)] = own[place]
        target[pl.ds(pl.multiple_of((1 - core) * COLS, COLS), COLS)] = arrived[place]
    worst = jnp.max(jnp.maximum(other[2 * COLS :], arrived[2 * COLS :]))
    bad[0] = (worst > 0.5).astype(jnp.int32)


def call(kernel, out_shape, smem, vmem, scratch=(), flops=10**6, out_specs=None):
    return pl.pallas_call(
        kernel,
        out_shape=out_shape,
        in_specs=[SMEM] * len(smem) + [VMEM] * len(vmem),
        out_specs=out_specs or jax.tree.map(lambda unused: VMEM, out_shape),
        scratch_shapes=scratch,
        compiler_params=PARAMS,
        cost_estimate=pl.CostEstimate(flops=flops, bytes_accessed=2**20, transcendentals=0),
    )(*smem, *vmem)


def exchanged_over(groups):
    def exchanged(value):
        return lax.all_to_all(value, "sub", 0, 0, axis_index_groups=groups)

    return exchanged


def swapped(value, first):
    subs = lax.axis_size("sub")
    pairs = [(i, (i + 1) % subs) for i in range(first, subs, 2)]
    return lax.ppermute(value, "sub", pairs + [(j, i) for i, j in pairs])


def sent_across(value):
    subs = lax.axis_size("sub")
    pairs = [(i, (i + 2 if i % 2 == 0 else i - 2) % subs) for i in range(subs)]
    return lax.ppermute(value, "sub", pairs)


def core_swapped(value):
    return lax.ppermute(value, "fold", [(0, 1), (1, 0), (2, 3), (3, 2)])


def passed(value, by):
    subs = lax.axis_size("sub")
    return lax.ppermute(value, "sub", [(i, (i + by) % subs) for i in range(subs)])


VECTOR = f32(COLS, ROWS)
HALO_PART = f32(COLS, HALO * BS)


def cycle_by_cycle(right_side, blocks, block_cols, lists):
    gathered = lax.all_gather(right_side, "fold", axis=0, tiled=True)

    def applied(vector):
        own = vector.reshape(NB, BS, -1)
        received = [passed(own[lists[0]], 1), passed(own[lists[1]], -1)]
        extended = jnp.concatenate([own, *received], 0)

        def added(slot, total):
            stored = lax.dynamic_index_in_dim(blocks, slot, 1, False)
            source = extended[lax.dynamic_index_in_dim(block_cols, slot, 1, False)]
            return total + jnp.einsum(
                "bij,bjc->bic", stored, source, precision=lax.Precision.HIGHEST
            )

        return lax.fori_loop(0, blocks.shape[1], added, jnp.zeros_like(own)).reshape(vector.shape)

    def grown(power, basis):
        latest = lax.dynamic_index_in_dim(basis, power, 0, False)
        following = (applied(latest) - CENTER * latest) / RADIUS
        return lax.dynamic_update_index_in_dim(basis, following, power + 1, 0)

    def cycle(unused, state):
        correction, residual = state
        basis = jnp.zeros((STEPS + 1,) + residual.shape, jnp.float32).at[0].set(residual)
        basis = lax.fori_loop(0, STEPS, grown, basis)
        gram = jnp.einsum("irc,jrc->ijc", basis, basis, precision=lax.Precision.HIGHEST)
        weights, left = solved_weights(lax.psum(gram, "sub"))
        correction = correction + sum(weights[i] * basis[i] for i in range(STEPS))
        return correction, sum(left[i] * basis[i] for i in range(STEPS + 1))

    fold = lax.axis_index("fold")
    results = lax.fori_loop(0, CYCLES, cycle, (jnp.zeros_like(gathered), gathered))
    return tuple(lax.dynamic_slice_in_dim(value, fold * BS, BS, 0).T for value in results)


def on_device(right_side, blocks, block_cols, send_lists):
    subs = lax.axis_size("sub")
    lists = send_lists[0]
    gathered = lax.all_gather(right_side.T, "fold", axis=1, tiled=True)
    operator = call(
        operator_kernel,
        (bf16(ROWS, ROWS),) * 6 + (f32(SHARED, BS),) * CHUNKS,
        [block_cols, lists],
        [blocks],
        [pltpu.VMEM((EXT * BS, ROWS), jnp.float32)],
        flops=10**9,
    )
    operator, chunks = operator[:6], operator[6:]
    masks_shape = f32(2, HALO, NB, SUBLANES, BS)
    masks, *sends = call(
        start_kernel, (masks_shape, VECTOR, HALO_PART, HALO_PART), [lists], [gathered]
    )
    square = f32(BS, BS)
    vectors, earlier, sums = [], [], []

    def own_part(vector):
        row = f32(len(vectors) + 1, SUBLANES, BS)
        partial, coarse, rest, high, low = call(
            round_kernel,
            (VECTOR, square, square, row, row),
            [],
            [vector, *operator[:3], *earlier],
            flops=10**9,
        )
        vectors.append(vector)
        earlier.extend([coarse, rest])
        sums.extend([high, low])
        return partial

    def stepped(partial, first, second):
        return list(
            call(
                step_kernel,
                (VECTOR, HALO_PART, HALO_PART),
                [],
                [masks, partial, first, second, *operator[3:]],
            )
        )

    shared = []
    for power in range(SINGLE):
        if power == SINGLE - 1:
            shared, sends[0] = lax.optimization_barrier((shared, sends[0]))
            others = [core_swapped(chunk) for chunk in shared]
        partial = own_part(sends[0])
        if power < 2:
            due = chunks[:1] if power == 0 else chunks[1:]
            due, partial = lax.optimization_barrier((due, partial))
            shared += [swapped(chunk, 1) for chunk in due]
        sends = stepped(partial, swapped(sends[1], 1), swapped(sends[2], 0))
    *ghost_operator, partner_masks = call(
        ghost_kernel,
        (bf16(EXT * BS, HALO * BS),) * 3 + (f32(HALO, NB, SUBLANES, BS),),
        [],
        [*shared, *others],
        flops=10**8,
    )
    for power in range(SINGLE, COUNT - 1, 2):
        vector, between, within = sends
        partial = own_part(vector)
        arrived = [swapped(vector, 1), sent_across(within), swapped(within, 0)]
        vector, within, ghost = call(
            ahead_kernel,
            (VECTOR, HALO_PART, HALO_PART),
            [],
            [masks, partner_masks, partial, *arrived, between, *operator[3:], *ghost_operator],
            [pltpu.VMEM((COLS, HALO * BS), jnp.float32)],
        )
        partial = own_part(vector)
        sends = stepped(partial, ghost, swapped(within, 0))
    vectors.append(sends[0])
    packed = f32(PART, 2 * SUM_ROWS, BS)
    sums = call(pack_kernel, packed, [], [vectors[-1], *earlier, *sums])
    strided = [[i + PART * j for j in range(subs // PART)] for i in range(PART)]
    runs = [[PART * i + j for j in range(PART)] for i in range(subs // PART)]
    sums = call(sum_kernel, packed, [], [exchanged_over(strided)(sums)])
    own, other = call(
        all_cycles_kernel,
        (f32(2 * COLS, BS), f32(2 * COLS + SUBLANES, BS)),
        [],
        [exchanged_over(runs)(sums), *vectors],
    )
    arrived = core_swapped(other)
    correction, residual, bad = call(
        join_kernel,
        (f32(2 * COLS, BS), f32(2 * COLS, BS), jax.ShapeDtypeStruct((1,), jnp.int32)),
        [],
        [own, other, arrived],
        out_specs=(VMEM, VMEM, SMEM),
    )
    correction, residual = lax.cond(
        bad[0] > 0,
        lambda correction, residual, *rest: cycle_by_cycle(*rest),
        lambda correction, residual, *rest: (correction, residual),
        correction,
        residual,
        right_side,
        blocks,
        block_cols,
        lists,
    )
    return (correction.T, residual.T)


def solution(mesh):
    placed = (
        P(("sub", "fold"), None),
        P("sub", None, None, None),
        P("sub", None),
        P("sub", None, None),
    )
    return jax.shard_map(
        on_device,
        mesh=mesh,
        in_specs=placed,
        out_specs=(P(("sub", "fold"), None), P(("sub", "fold"), None)),
        check_vma=False,
    )
```

```python
import functools

import jax
import jax.numpy as jnp
from jax import lax
from jax.experimental import pallas as pl
from jax.experimental.pallas import tpu as pltpu
from jax.sharding import PartitionSpec as P

STEPS = 4
CYCLES = 3
CENTER = 4.5
RADIUS = 3.5
BS = 128
NB = 4
HALO = 2
EXT = NB + 2 * HALO
ROWS = NB * BS
COLS = 32
PAIRS = [(i, j) for i in range(STEPS + 1) for j in range(i, STEPS + 1)]
GROUP = 128 // COLS
GRAM_ROWS = (len(PAIRS) + GROUP - 1) // GROUP

COUNT = STEPS * CYCLES + 1
SUBLANES = 8
PART = 8
TILES = -(-COUNT * (COUNT + 1) // 2 // (SUBLANES * GROUP))
SUM_ROWS = TILES * SUBLANES
LIMIT = 2000.0
SINGLE = 4
CHUNKS = SINGLE - 1
SHARED = (EXT * BS + NB * SUBLANES) // CHUNKS

VMEM = pl.BlockSpec(memory_space=pltpu.VMEM)
SMEM = pl.BlockSpec(memory_space=pltpu.SMEM)
PARAMS = pltpu.CompilerParams(vmem_limit_bytes=32 * 1024 * 1024)


def f32(*shape):
    return jax.ShapeDtypeStruct(shape, jnp.float32)


def bf16(*shape):
    return jax.ShapeDtypeStruct(shape, jnp.bfloat16)


def split(value):
    high = value.astype(jnp.bfloat16)
    value = value - high.astype(jnp.float32)
    middle = value.astype(jnp.bfloat16)
    low = (value - middle.astype(jnp.float32)).astype(jnp.bfloat16)
    return high, middle, low


def product(vector, high, middle, low):
    parts = split(vector)
    first = jnp.dot(
        jnp.concatenate(parts, 0), high[...], preferred_element_type=jnp.float32
    )
    second = jnp.dot(
        jnp.concatenate(parts[:2], 0), middle[...], preferred_element_type=jnp.float32
    )
    third = jnp.dot(parts[0], low[...], preferred_element_type=jnp.float32)
    small = first[2 * COLS :] + second[COLS:] + third
    return first[:COLS] + (first[COLS : 2 * COLS] + second[:COLS] + small)


def sent_block(lists, side, slot):
    return lists[(side + lax.axis_index("sub") + 1) % 2, slot]


def chosen_block(listed, block):
    return jnp.where(jnp.full((SUBLANES, BS), listed, jnp.int32) == block, 1.0, 0.0)


def operator_kernel(cols, lists, blocks, *refs):
    own, received, chunks, dense = refs[:3], refs[3:6], refs[6:-1], refs[-1]
    turn = HALO * (lax.axis_index("sub") % 2)
    dense[...] = jnp.zeros_like(dense)
    for row in range(NB):
        for slot in range(blocks.shape[1]):
            column = cols[row, slot]
            swapped = NB + (column - NB + turn) % (2 * HALO)
            start = pl.multiple_of(jnp.where(column < NB, column, swapped) * BS, BS)
            place = (pl.ds(start, BS), slice(row * BS, (row + 1) * BS))
            dense[place] = dense[place] + blocks[row, slot].T
    unit = (
        lax.broadcasted_iota(jnp.int32, (BS, BS), 0) == lax.broadcasted_iota(jnp.int32, (BS, BS), 1)
    ).astype(jnp.float32)
    for row in range(NB):
        for column in range(EXT):
            place = (slice(column * BS, (column + 1) * BS), slice(row * BS, (row + 1) * BS))
            value = dense[place]
            if row == column:
                value = value - CENTER * unit
            value = value * (1.0 / RADIUS)
            dense[place] = value
            targets = own if column < NB else received
            start = (column % NB) * BS
            for target, part in zip(targets, split(value)):
                target[start : start + BS, row * BS : (row + 1) * BS] = part
    listed = sent_block(lists, 0, lax.axis_index("fold") % 2)
    masks = [chosen_block(listed, block) for block in range(NB)]
    start = pl.multiple_of(listed * BS, BS)
    shared = jnp.concatenate([dense[:, pl.ds(start, BS)], *masks], 0)
    for index, chunk in enumerate(chunks):
        chunk[...] = shared[index * SHARED : (index + 1) * SHARED]


def ghost_kernel(*refs):
    mine, others = (
        jnp.concatenate([ref[...] for ref in half], 0)
        for half in (refs[:CHUNKS], refs[CHUNKS : 2 * CHUNKS])
    )
    parts, masks = refs[2 * CHUNKS : -1], refs[-1]
    even = lax.axis_index("fold") % 2 == 0
    for slot in range(HALO):
        one, other = (mine, others) if slot == 0 else (others, mine)
        value = jnp.where(even, one, other)
        place = slice(slot * BS, (slot + 1) * BS)
        for target, part in zip(parts, split(value[: EXT * BS])):
            target[:, place] = part
        for block in range(NB):
            start = EXT * BS + block * SUBLANES
            masks[slot, block] = value[start : start + SUBLANES]


def write_chosen(masks, vector, target):
    repeats = vector.shape[0] // SUBLANES
    for slot in range(HALO):
        total = None
        for block in range(NB):
            mask = jnp.concatenate([masks[slot, block]] * repeats, 0)
            value = vector[:, block * BS : (block + 1) * BS]
            total = value if total is None else jnp.where(mask > 0.5, value, total)
        target[:, slot * BS : (slot + 1) * BS] = total


def write_sends(masks, vector, sends):
    for side, target in enumerate(sends):
        write_chosen(masks.at[side], vector, target)


def start_kernel(lists, gathered, masks, result, *sends):
    first = pl.multiple_of(lax.axis_index("fold") % 2 * COLS, COLS)
    for side in range(2):
        for slot in range(HALO):
            listed = sent_block(lists, side, slot)
            for block in range(NB):
                masks[side, slot, block] = chosen_block(listed, block)
    vector = gathered[pl.ds(first, COLS), :]
    result[...] = vector
    write_sends(masks, vector, sends)


def step_kernel(masks, partial, first, second, *refs):
    parts, (result, *sends) = refs[:3], refs[3:]
    received = jnp.concatenate([first[...], second[...]], 1)
    vector = partial[...] + product(received, *parts)
    result[...] = vector
    write_sends(masks, vector, sends)


def ahead_kernel(masks, partner_masks, partial, whole, across, near, sent, *refs):
    parts, ghost_parts, (result, send, ghost, first) = refs[:3], refs[3:6], refs[6:]
    write_chosen(partner_masks, whole, first)
    received = jnp.concatenate([first[...], near[...]], 1)
    vector = partial[...] + product(received, *parts)
    result[...] = vector
    write_chosen(masks.at[1], vector, send)
    extended = jnp.concatenate([whole[...], sent[...], across[...]], 1)
    ghost[...] = product(extended, *ghost_parts)


def small_solve(matrix, target):
    count = len(target)
    lower = [[None] * count for unused in range(count)]
    inverse = [None] * count
    for outer in range(count):
        for inner in range(outer + 1):
            total = matrix[outer][inner]
            for other in range(inner):
                total = total - lower[outer][other] * lower[inner][other]
            if outer == inner:
                inverse[outer] = 1.0 / jnp.sqrt(total)
            else:
                lower[outer][inner] = total * inverse[inner]
    solved = []
    for outer in range(count):
        total = target[outer]
        for other in range(outer):
            total = total - lower[outer][other] * solved[other]
        solved.append(total * inverse[outer])
    result = [None] * count
    for outer in reversed(range(count)):
        total = solved[outer]
        for other in range(outer + 1, count):
            total = total - lower[other][outer] * result[other]
        result[outer] = total * inverse[outer]
    return result


def two_sum(left, right):
    total = left + right
    shadow = total - left
    return total, (left - (total - shadow)) + (right - shadow)


def coarse_split(value):
    grid = jnp.max(jnp.abs(value), 0, keepdims=True) * (1.5 * 2.0**15)
    coarse = (value + grid) - grid
    return coarse, value - coarse


def gram_row(vector, earlier):
    turned = jnp.concatenate([vector[:, i * BS : (i + 1) * BS] for i in range(NB)], 0).T
    coarse, rest = coarse_split(turned)
    row = []
    for other, other_rest in [*earlier, (coarse, rest)]:
        high = low = None
        for start in range(0, BS, SUBLANES):
            place = slice(start, start + SUBLANES)
            main = other[place] * coarse[place]
            side = other[place] * rest[place] + other_rest[place] * turned[place]
            high = main if high is None else high + main
            low = side if low is None else low + side
        row.append((high, low))
    return coarse, rest, row


def round_kernel(*refs):
    vector, parts, earlier = refs[0], refs[1:4], refs[4:-5]
    partial, coarse, rest, high, low = refs[-5:]
    value = vector[...]
    partial[...] = product(value, *parts)
    earlier = [(earlier[i], earlier[i + 1]) for i in range(0, len(earlier), 2)]
    coarse[...], rest[...], row = gram_row(value, earlier)
    for index, (one, other) in enumerate(row):
        high[index], low[index] = one, other


def pack_kernel(*refs):
    vector, earlier = refs[0], refs[1 : 1 + 2 * (COUNT - 1)]
    sums, packed = refs[1 + 2 * (COUNT - 1) : -1], refs[-1]
    earlier = [(earlier[i], earlier[i + 1]) for i in range(0, len(earlier), 2)]
    pairs = []
    for index in range(0, len(sums), 2):
        for i in range(sums[index].shape[0]):
            pairs.append((sums[index][i], sums[index + 1][i]))
    pairs += gram_row(vector[...], earlier)[2]
    sublane = lax.broadcasted_iota(jnp.int32, (SUBLANES, BS), 0)
    lane = lax.broadcasted_iota(jnp.int32, (SUBLANES, BS), 1) // COLS

    def folded(high, low, shift, axis):
        high, error = two_sum(high, pltpu.roll(high, shift, axis))
        return high, low + pltpu.roll(low, shift, axis) + error

    zero = jnp.zeros((SUBLANES, BS), jnp.float32)
    for tile in range(TILES):
        tile_high, tile_low = zero, zero
        for group in range(GROUP):
            high, low = zero, zero
            for row in range(SUBLANES):
                index = (tile * GROUP + group) * SUBLANES + row
                if index < len(pairs):
                    one, other = pairs[index]
                    for shift in (4, 2, 1):
                        one, other = folded(one, other, shift, 0)
                    high = jnp.where(sublane == row, one, high)
                    low = jnp.where(sublane == row, other, low)
            for shift in (2 * COLS, COLS):
                high, low = folded(high, low, shift, 1)
            tile_high = jnp.where(lane == group, high, tile_high)
            tile_low = jnp.where(lane == group, low, tile_low)
        tile_high, tile_low = two_sum(tile_high, tile_low)
        for copy in range(PART):
            packed[copy, tile * SUBLANES : (tile + 1) * SUBLANES] = tile_high
            packed[copy, SUM_ROWS + tile * SUBLANES : SUM_ROWS + (tile + 1) * SUBLANES] = tile_low


def summed(parts):
    high, low = parts[0, :SUM_ROWS], parts[0, SUM_ROWS:]
    for index in range(1, PART):
        high, error = two_sum(high, parts[index, :SUM_ROWS])
        low = low + parts[index, SUM_ROWS:] + error
    return two_sum(high, low)


def sum_kernel(parts, total):
    high, low = summed(parts)
    for copy in range(PART):
        total[copy, :SUM_ROWS] = high
        total[copy, SUM_ROWS:] = low


def halves(value):
    scaled = value * 4097.0
    high = scaled - (scaled - value)
    return high, value - high


def added_product(total, factor, value):
    factor, factor_high, factor_low = factor
    value, low, value_high, value_low = value
    main = factor_high * value_high
    side = factor_high * value_low + (factor_low * value + factor * low)
    if total is None:
        return main, side
    high, error = two_sum(total[0], main)
    return high, total[1] + (error + side)


def basis_gram(coefficients, gram):
    depth = gram[0][0].shape[0]
    index = lax.broadcasted_iota(jnp.int32, (depth, BS), 0)
    wide = [jnp.concatenate([value] * (depth // SUBLANES), 0) for value in coefficients]
    factors = [(value, *halves(value)) for value in wide]
    rows = []
    for i in range(STEPS + 1):
        total = None
        for a, factor in enumerate(factors):
            total = added_product(total, factor, gram[a + i])
        high, low = two_sum(*total)
        rows.append((high, low, *halves(high)))
    result = [[None] * (STEPS + 1) for unused in range(STEPS + 1)]
    for j in range(STEPS + 1):
        shifted = jnp.zeros((depth, BS), jnp.float32)
        for a, value in enumerate(wide):
            shifted = jnp.where(index == a + j, value, shifted)
        factor = (shifted, *halves(shifted))
        for i in range(j + 1):
            high, low = added_product(None, factor, rows[i])
            size = depth
            while size > SUBLANES:
                size //= 2
                high, error = two_sum(high[:size], high[size:])
                low = low[:size] + low[size:] + error
            for shift in (4, 2, 1):
                high, error = two_sum(high, pltpu.roll(high, shift, 0))
                low = low + pltpu.roll(low, shift, 0) + error
            result[i][j] = result[j][i] = high + low
    return result


def solved_weights(gram):
    combined = [
        [CENTER * gram[i][j] + RADIUS * gram[i + 1][j] for j in range(STEPS + 1)]
        for i in range(STEPS)
    ]
    normal = [
        [CENTER * combined[i][j] + RADIUS * combined[i][j + 1] for j in range(STEPS)]
        for i in range(STEPS)
    ]
    weights = small_solve(normal, [combined[i][0] for i in range(STEPS)])
    left = [1.0 - CENTER * weights[0]]
    for i in range(1, STEPS):
        left.append(-(CENTER * weights[i] + RADIUS * weights[i - 1]))
    left.append(-(RADIUS * weights[STEPS - 1]))
    return weights, left


def convolved(left, right):
    result = [None] * (len(left) + len(right) - 1)
    for i, one in enumerate(left):
        for j, other in enumerate(right):
            term = one * other
            result[i + j] = term if result[i + j] is None else result[i + j] + term
    return result


def all_cycles_kernel(parts, *refs):
    vectors, own, other = refs[:COUNT], refs[COUNT], refs[COUNT + 1]
    high, low = summed(parts)
    rolled = [(high, low)]
    for group in range(1, GROUP):
        shift = BS - group * COLS
        rolled.append((pltpu.roll(high, shift, 1), pltpu.roll(low, shift, 1)))

    def entry(i, j):
        index = max(i, j) * (max(i, j) + 1) // 2 + min(i, j)
        tile, rest = divmod(index, SUBLANES * GROUP)
        group, row = divmod(rest, SUBLANES)
        row += tile * SUBLANES
        return [value[row : row + 1] for value in rolled[group]]

    depth = 2 * SUBLANES
    padding = [jnp.zeros((depth - COUNT, BS), jnp.float32)]
    gram = []
    for i in range(COUNT):
        entries = [entry(i, j) for j in range(COUNT)]
        value = jnp.concatenate([one for one, unused in entries] + padding, 0)
        rest = jnp.concatenate([one for unused, one in entries] + padding, 0)
        gram.append((value, rest, *halves(value)))

    def spread(value):
        return jnp.broadcast_to(value, (SUBLANES, BS))

    here = [[spread(entry(i, j)[0]) for j in range(STEPS + 1)] for i in range(STEPS + 1)]
    weights, polynomial = solved_weights(here)
    solution_part = list(weights)
    for cycle in range(1, CYCLES):
        here = basis_gram(polynomial, gram)
        weights, left = solved_weights(here)
        update = convolved(polynomial, weights)
        solution_part = [
            one + solution_part[i] if i < len(solution_part) else one
            for i, one in enumerate(update)
        ]
        polynomial = convolved(polynomial, left)
    remaining = None
    for i in range(STEPS + 1):
        for j in range(STEPS + 1):
            term = (left[i] * left[j]) * here[i][j]
            remaining = term if remaining is None else remaining + term
    reach = None
    for i in range(COUNT):
        term = jnp.abs(polynomial[i]) * jnp.sqrt(spread(entry(i, i)[0]))
        reach = term if reach is None else reach + term
    lane = lax.broadcasted_iota(jnp.int32, (SUBLANES, BS), 1)
    fine = (reach < LIMIT * jnp.sqrt(remaining)) | (lane >= COLS)
    bad = jnp.max(jnp.where(fine, 0.0, 1.0), axis=(0, 1), keepdims=True)
    other[2 * COLS :] = jnp.broadcast_to(bad, (SUBLANES, BS))
    index = lax.broadcasted_iota(jnp.int32, (depth, BS), 0)
    stacked = []
    for values in (solution_part, polynomial):
        total = jnp.zeros((depth, BS), jnp.float32)
        for i, value in enumerate(values):
            value = jnp.concatenate([value] * (depth // SUBLANES), 0)
            total = jnp.where(index == i, value, total)
        stacked.append(total)
    turned = jnp.concatenate(stacked, 0).T
    place = lax.axis_index("fold")
    partner = place + 1 - 2 * (place % 2)
    for output in range(2):
        sums = [None, None]
        for i in range(COUNT - 1 + output):
            column = output * depth + i
            weight = jnp.broadcast_to(turned[:COLS, column : column + 1], (COLS, BS))
            for side, block in enumerate((place, partner)):
                value = vectors[i][:, pl.ds(pl.multiple_of(block * BS, BS), BS)]
                term = weight * value
                sums[side] = term if sums[side] is None else sums[side] + term
        own[output * COLS : (output + 1) * COLS] = sums[0]
        other[output * COLS : (output + 1) * COLS] = sums[1]


def join_kernel(own, other, arrived, correction, residual, bad):
    core = lax.axis_index("fold") % 2
    for output, target in enumerate((correction, residual)):
        place = slice(output * COLS, (output + 1) * COLS)
        target[pl.ds(pl.multiple_of(core * COLS, COLS), COLS)] = own[place]
        target[pl.ds(pl.multiple_of((1 - core) * COLS, COLS), COLS)] = arrived[place]
    worst = jnp.max(jnp.maximum(other[2 * COLS :], arrived[2 * COLS :]))
    bad[0] = (worst > 0.5).astype(jnp.int32)


def call(kernel, out_shape, smem, vmem, scratch=(), flops=10**6, out_specs=None):
    return pl.pallas_call(
        kernel,
        out_shape=out_shape,
        in_specs=[SMEM] * len(smem) + [VMEM] * len(vmem),
        out_specs=out_specs or jax.tree.map(lambda unused: VMEM, out_shape),
        scratch_shapes=scratch,
        compiler_params=PARAMS,
        cost_estimate=pl.CostEstimate(flops=flops, bytes_accessed=2**20, transcendentals=0),
    )(*smem, *vmem)


def exchanged_over(groups):
    def exchanged(value):
        return lax.all_to_all(value, "sub", 0, 0, axis_index_groups=groups)

    return exchanged


def swapped(value, first):
    subs = lax.axis_size("sub")
    pairs = [(i, (i + 1) % subs) for i in range(first, subs, 2)]
    return lax.ppermute(value, "sub", pairs + [(j, i) for i, j in pairs])


def sent_across(value):
    subs = lax.axis_size("sub")
    pairs = [(i, (i + 2 if i % 2 == 0 else i - 2) % subs) for i in range(subs)]
    return lax.ppermute(value, "sub", pairs)


def core_swapped(value):
    return lax.ppermute(value, "fold", [(0, 1), (1, 0), (2, 3), (3, 2)])


def passed(value, by):
    subs = lax.axis_size("sub")
    return lax.ppermute(value, "sub", [(i, (i + by) % subs) for i in range(subs)])


VECTOR = f32(COLS, ROWS)
HALO_PART = f32(COLS, HALO * BS)


def cycle_by_cycle(right_side, blocks, block_cols, lists):
    gathered = lax.all_gather(right_side, "fold", axis=0, tiled=True)

    def applied(vector):
        own = vector.reshape(NB, BS, -1)
        received = [passed(own[lists[0]], 1), passed(own[lists[1]], -1)]
        extended = jnp.concatenate([own, *received], 0)

        def added(slot, total):
            stored = lax.dynamic_index_in_dim(blocks, slot, 1, False)
            source = extended[lax.dynamic_index_in_dim(block_cols, slot, 1, False)]
            return total + jnp.einsum(
                "bij,bjc->bic", stored, source, precision=lax.Precision.HIGHEST
            )

        return lax.fori_loop(0, blocks.shape[1], added, jnp.zeros_like(own)).reshape(vector.shape)

    def grown(power, basis):
        latest = lax.dynamic_index_in_dim(basis, power, 0, False)
        following = (applied(latest) - CENTER * latest) / RADIUS
        return lax.dynamic_update_index_in_dim(basis, following, power + 1, 0)

    def cycle(unused, state):
        correction, residual = state
        basis = jnp.zeros((STEPS + 1,) + residual.shape, jnp.float32).at[0].set(residual)
        basis = lax.fori_loop(0, STEPS, grown, basis)
        gram = jnp.einsum("irc,jrc->ijc", basis, basis, precision=lax.Precision.HIGHEST)
        weights, left = solved_weights(lax.psum(gram, "sub"))
        correction = correction + sum(weights[i] * basis[i] for i in range(STEPS))
        return correction, sum(left[i] * basis[i] for i in range(STEPS + 1))

    fold = lax.axis_index("fold")
    results = lax.fori_loop(0, CYCLES, cycle, (jnp.zeros_like(gathered), gathered))
    return tuple(lax.dynamic_slice_in_dim(value, fold * BS, BS, 0).T for value in results)


def on_device(right_side, blocks, block_cols, send_lists):
    subs = lax.axis_size("sub")
    lists = send_lists[0]
    gathered = lax.all_gather(right_side.T, "fold", axis=1, tiled=True)
    operator = call(
        operator_kernel,
        (bf16(ROWS, ROWS),) * 6 + (f32(SHARED, BS),) * CHUNKS,
        [block_cols, lists],
        [blocks],
        [pltpu.VMEM((EXT * BS, ROWS), jnp.float32)],
        flops=10**9,
    )
    operator, chunks = operator[:6], operator[6:]
    masks_shape = f32(2, HALO, NB, SUBLANES, BS)
    masks, *sends = call(
        start_kernel, (masks_shape, VECTOR, HALO_PART, HALO_PART), [lists], [gathered]
    )
    square = f32(BS, BS)
    vectors, earlier, sums = [], [], []

    def own_part(vector):
        row = f32(len(vectors) + 1, SUBLANES, BS)
        partial, coarse, rest, high, low = call(
            round_kernel,
            (VECTOR, square, square, row, row),
            [],
            [vector, *operator[:3], *earlier],
            flops=10**9,
        )
        vectors.append(vector)
        earlier.extend([coarse, rest])
        sums.extend([high, low])
        return partial

    def stepped(partial, first, second, last=False):
        return list(
            call(
                step_kernel,
                (VECTOR,) if last else (VECTOR, HALO_PART, HALO_PART),
                [],
                [masks, partial, first, second, *operator[3:]],
            )
        )

    shared = []
    for power in range(SINGLE):
        if power < CHUNKS:
            chunk, partial = lax.optimization_barrier((chunks[power], own_part(sends[0])))
            shared.append(swapped(chunk, 1))
        else:
            shared, sends[0] = lax.optimization_barrier((shared, sends[0]))
            others = [core_swapped(chunk) for chunk in shared]
            partial = own_part(sends[0])
        sends = stepped(partial, swapped(sends[1], 1), swapped(sends[2], 0))
    *ghost_operator, partner_masks = call(
        ghost_kernel,
        (bf16(EXT * BS, HALO * BS),) * 3 + (f32(HALO, NB, SUBLANES, BS),),
        [],
        [*shared, *others],
        flops=10**8,
    )
    for power in range(SINGLE, COUNT - 1, 2):
        vector, between, within = sends
        partial = own_part(vector)
        arrived = [swapped(vector, 1), sent_across(within), swapped(within, 0)]
        vector, within, ghost = call(
            ahead_kernel,
            (VECTOR, HALO_PART, HALO_PART),
            [],
            [masks, partner_masks, partial, *arrived, between, *operator[3:], *ghost_operator],
            [pltpu.VMEM((COLS, HALO * BS), jnp.float32)],
        )
        partial = own_part(vector)
        sends = stepped(partial, ghost, swapped(within, 0), power + 2 == COUNT - 1)
    vectors.append(sends[0])
    packed = f32(PART, 2 * SUM_ROWS, BS)
    sums = call(pack_kernel, packed, [], [vectors[-1], *earlier, *sums])
    strided = [[i + PART * j for j in range(subs // PART)] for i in range(PART)]
    runs = [[PART * i + j for j in range(PART)] for i in range(subs // PART)]
    sums = call(sum_kernel, packed, [], [exchanged_over(strided)(sums)])
    own, other = call(
        all_cycles_kernel,
        (f32(2 * COLS, BS), f32(2 * COLS + SUBLANES, BS)),
        [],
        [exchanged_over(runs)(sums), *vectors],
    )
    arrived = core_swapped(other)
    correction, residual, bad = call(
        join_kernel,
        (f32(2 * COLS, BS), f32(2 * COLS, BS), jax.ShapeDtypeStruct((1,), jnp.int32)),
        [],
        [own, other, arrived],
        out_specs=(VMEM, VMEM, SMEM),
    )
    correction, residual = lax.cond(
        bad[0] > 0,
        lambda correction, residual, *rest: cycle_by_cycle(*rest),
        lambda correction, residual, *rest: (correction, residual),
        correction,
        residual,
        right_side,
        blocks,
        block_cols,
        lists,
    )
    return (correction.T, residual.T)


def solution(mesh):
    placed = (
        P(("sub", "fold"), None),
        P("sub", None, None, None),
        P("sub", None),
        P("sub", None, None),
    )
    return jax.shard_map(
        on_device,
        mesh=mesh,
        in_specs=placed,
        out_specs=(P(("sub", "fold"), None), P(("sub", "fold"), None)),
        check_vma=False,
    )
```
